256 devices in a mesh: dp: 8 (over x, core), mp: 32 (over z, y).
Axes of the slice: x: 4, y: 4, z: 8, core: 2. Of those that a mesh axis runs over, the one named last changes fastest.
Arguments:
- tokens: bfloat16 [8192, 8192], P('dp', 'mp'), may hold values from -6 to 6
- cotangent: bfloat16 [8192, 14336], P('dp', 'mp'), may hold values from -0.1875 to 0.1875
- frozen_up_weight: bfloat16 [8192, 14336], P(None, 'mp'), may hold values from -0.0625 to 0.0625
- down_factors: bfloat16 [64, 8192, 64], P('dp', 'mp'), may hold values from -0.0625 to 0.0625
- up_factors: bfloat16 [64, 64, 14336], P('dp', None, 'mp'), may hold values from -0.75 to 0.75
- used: int32 [8, 8], P('dp'), may hold values from 0 to 63, as said below
- sequence_slot: int32 [8, 8], P('dp'), may hold values from 0 to 7, each once within a row
Outputs:
- adjusted_projection: bfloat16 [8192, 14336], P('dp', 'mp')
- grad_a: float32 [64, 8192, 64], P('dp', 'mp')
- grad_b: float32 [64, 64, 14336], P('dp', None, 'mp')
The draws below stay inside these ranges and needn't reach their ends.
Inputs may be any that keep to these rules, and one draw needn't show every extreme that they name: `used`: each row holds 8 distinct adapters; from the 8 adapters k*8 to (k+1)*8 - 1 of one index k of dp a row takes none or exactly 2.
All inputs are finite; a program needn't handle non-finite values.
Results may differ from the reference program's by a relative error of at most 0.0075.
Values may be sent and summed in bfloat16 or wider, within the bound.
No kernel may reach another device: no remote copies, remote signals or barrier semaphores. Data moves between devices by JAX's collectives and lax.ppermute only.
A program may use at most 128 MiB of HBM per device.

```python
import jax
import jax.numpy as jnp
from jax import lax

MODEL_WIDTH = 8192
HIDDEN_UNITS = 14336
ADAPTER_RANK = 64
AD_DEV = 8
MOST = 2
USE = 8
LEN = 128
ADAPTER_TOTAL = 64
TOKENS = 8192
N_DP = 8


def draw_used(key, part):
    key = jax.random.fold_in(key, 3)
    group_keys = jax.random.split(key, N_DP)
    pair_count = USE // MOST

    def single_group(group_key):
        owner_key, pick_key = jax.random.split(group_key)
        owners = jax.random.permutation(owner_key, N_DP)
        pair_keys = jax.random.split(pick_key, pair_count)
        picks = jax.vmap(lambda pair_key: jax.random.permutation(pair_key, AD_DEV)[:MOST])(pair_keys)
        return (owners[:pair_count][:, None] * AD_DEV + picks).reshape(USE).astype(jnp.int32)
    return jax.vmap(single_group)(group_keys)


def steps_of(key, extent, cuts, smallest, high):
    level, own = 1.0, jax.random.fold_in(key, 6)
    for dim, shards_of in cuts:
        heights = jnp.exp(jax.random.uniform(jax.random.fold_in(own, dim), (shards_of,), jnp.float32, smallest / len(cuts), high / len(cuts)))
        level = level * jnp.repeat(heights, extent[dim] // shards_of).reshape([-1 if axis == dim else 1 for axis in range(len(extent))])
    return level


def normal_values(key, extent, scale, most, pieces=(), kind=jnp.bfloat16):
    entries = scale * jax.random.normal(key, extent, jnp.float32)
    if pieces:
        entries = entries * steps_of(key, extent, pieces, -0.22, 0.18)
    return jnp.clip(entries, -most, most).astype(kind)


def setup_inputs(seed: int = 0) -> dict:
    key_list = jax.random.split(jax.random.key(seed), 8)
    return {
        "tokens": normal_values(key_list[0], (TOKENS, MODEL_WIDTH), 1.0, 6.0, ((0, 8), (1, 32))),
        "cotangent": normal_values(key_list[1], (TOKENS, HIDDEN_UNITS), (2 * (ADAPTER_RANK / HIDDEN_UNITS) ** 0.5 / LEN ** 0.5), 0.1875, ((0, 8), (1, 32))),
        "frozen_up_weight": normal_values(key_list[2], (MODEL_WIDTH, HIDDEN_UNITS), MODEL_WIDTH ** -0.5, 0.0625, ((1, 32),)),
        "down_factors": normal_values(key_list[3], (ADAPTER_TOTAL, MODEL_WIDTH, ADAPTER_RANK), MODEL_WIDTH ** -0.5, 0.0625, ((0, 8), (1, 32))),
        "up_factors": normal_values(key_list[4], (ADAPTER_TOTAL, ADAPTER_RANK, HIDDEN_UNITS), ADAPTER_RANK ** -0.5, 0.75, ((0, 8), (2, 32))),
        "used": draw_used(jax.random.fold_in(key_list[7], 71), 0),
        "sequence_slot": jax.vmap(lambda own: jax.random.permutation(own, USE))(jax.random.split(key_list[6], N_DP)).reshape((N_DP, USE)).astype(jnp.int32),
    }


BLEND_MULTIPLIER = 2.0


def reference(tokens, cotangent, frozen_up_weight, down_factors, up_factors, used, sequence_slot):
    fixed_projection_result = jnp.dot(tokens, frozen_up_weight, preferred_element_type=jnp.float32)
    adapter_ids = jnp.take_along_axis(used, sequence_slot, axis=1).reshape(-1).astype(jnp.int32)
    seq_count = adapter_ids.shape[0]
    token_seq = tokens.reshape(seq_count, LEN, MODEL_WIDTH)
    cot_seq = cotangent.reshape(seq_count, LEN, HIDDEN_UNITS)
    base_seq = fixed_projection_result.reshape(seq_count, LEN, HIDDEN_UNITS)

    def one_sequence(seq_items):
        seq_rows, series_gradients, series_fixed, sequence_adapter = seq_items
        down_matrix = down_factors[sequence_adapter]
        raising_array = up_factors[sequence_adapter]
        activation_entries = jnp.dot(seq_rows, down_matrix, preferred_element_type=jnp.float32).astype(jnp.bfloat16)
        series_result = (series_fixed + BLEND_MULTIPLIER * jnp.dot(activation_entries, raising_array, preferred_element_type=jnp.float32)).astype(jnp.bfloat16)
        series_returned = (BLEND_MULTIPLIER * lax.dot_general(series_gradients, raising_array, (((1,), (1,)), ((), ())), preferred_element_type=jnp.float32)).astype(jnp.bfloat16)
        term_a = lax.dot_general(seq_rows, series_returned, (((0,), (0,)), ((), ())), preferred_element_type=jnp.float32)
        second_addend = BLEND_MULTIPLIER * lax.dot_general(activation_entries, series_gradients, (((0,), (0,)), ((), ())), preferred_element_type=jnp.float32)
        return series_result, term_a.astype(jnp.bfloat16), second_addend.astype(jnp.bfloat16)

    outputs, grads_a, grads_b = lax.map(one_sequence, (token_seq, cot_seq, base_seq, adapter_ids))
    grads_a = lax.optimization_barrier(grads_a).astype(jnp.float32)
    grads_b = lax.optimization_barrier(grads_b).astype(jnp.float32)
    grad_a = jax.ops.segment_sum(grads_a, adapter_ids, num_segments=ADAPTER_TOTAL)
    grad_b = jax.ops.segment_sum(grads_b, adapter_ids, num_segments=ADAPTER_TOTAL)
    return outputs.reshape(TOKENS, HIDDEN_UNITS), grad_a, grad_b
```

```python
import functools

import jax
import jax.numpy as jnp
from jax import lax
from jax.experimental import pallas as pl
from jax.experimental.pallas import tpu as pltpu
from jax.sharding import Mesh, PartitionSpec as P

BF = jnp.bfloat16
F32 = jnp.float32
DP = ("x", "core")
MP = ("z", "y")
VMEM = pl.BlockSpec(memory_space=pltpu.VMEM)
SMEM = pl.BlockSpec(memory_space=pltpu.SMEM)
LIMIT = 40 * 1024 * 1024


def pair_of(used, group, owner, per_owner, slots):
    low, high = jnp.int32(per_owner), jnp.int32(-1)
    for slot in range(slots):
        local = used[group, slot] - owner * per_owner
        inside = jnp.logical_and(local >= 0, local < per_owner)
        low = jnp.where(inside, jnp.minimum(low, local), low)
        high = jnp.where(inside, jnp.maximum(high, local), high)
    return low, high


def place_of(used, order, sequence, per_owner, slots):
    adapter = used[0, order[0, sequence]]
    owner = lax.div(adapter, jnp.int32(per_owner))
    second = jnp.int32(0)
    for slot in range(slots):
        other = used[0, slot]
        same = jnp.logical_and(lax.div(other, jnp.int32(per_owner)) == owner, other < adapter)
        second = jnp.where(same, jnp.int32(1), second)
    return owner * 2 + second


def pick_kernel(me, used, down, up, out):
    groups, slots = used.shape
    per_owner, rank, width = down.shape
    units = up.shape[2]
    for group in range(groups):
        low, high = pair_of(used, group, me[0], per_owner, slots)
        for place, local in ((0, low), (1, high)):
            index = jnp.clip(local, 0, per_owner - 1)
            out[group, place, :, 0:width] = down[index]
            out[group, place, :, width:width + units] = up[index]
            out[group, place, :, width + units:] = jnp.zeros((rank, out.shape[3] - width - units), BF)


def parts_kernel(used, order, factors, tokens, cot, out, *, rank, width, units):
    sequences = order.shape[1]
    length = tokens.shape[0] // sequences
    per_owner = sequences
    for i in range(sequences):
        place = place_of(used, order, i, per_owner, used.shape[1])
        own = factors[place]
        rows = tokens[i * length:(i + 1) * length, :]
        inputs = lax.dot_general(
            own[:, 0:width], rows, (((1,), (1,)), ((), ())), preferred_element_type=F32
        )
        back = 2.0 * jnp.dot(
            own[:, width:width + units],
            cot[:, i * length:(i + 1) * length],
            preferred_element_type=F32,
        )
        both = jnp.concatenate([inputs, back], axis=0)
        out[i * length:(i + 1) * length, :] = both.T.astype(BF)


def grads_kernel(used, order, factors, tokens, cot, both, send, delta, *, rank, width, units):
    sequences = order.shape[1]
    length = tokens.shape[0] // sequences
    per_owner = sequences
    send[...] = jnp.zeros(send.shape, BF)
    for i in range(sequences):
        place = place_of(used, order, i, per_owner, used.shape[1])
        span = slice(i * length, (i + 1) * length)
        turned = both[span, :].astype(F32).T.astype(BF)
        inputs, back = turned[0:rank, :], turned[rank:2 * rank, :]
        term_a = jnp.dot(back, tokens[span, :], preferred_element_type=F32)
        term_b = 2.0 * lax.dot_general(
            inputs, cot[:, span], (((1,), (1,)), ((), ())), preferred_element_type=F32
        )
        send[place, :, 0:width] = term_a.astype(BF)
        send[place, :, width:width + units] = term_b.astype(BF)
        up = factors[place][:, width:width + units]
        delta[:, span] = 2.0 * lax.dot_general(
            up, inputs, (((0,), (0,)), ((), ())), preferred_element_type=F32
        )


def sum_kernel(me, used, terms, grad_a, grad_b):
    groups, slots = used.shape
    per_owner, rank, width = grad_a.shape
    units = grad_b.shape[2]
    grad_a[...] = jnp.zeros(grad_a.shape, F32)
    grad_b[...] = jnp.zeros(grad_b.shape, F32)
    for group in range(groups):
        low, high = pair_of(used, group, me[0], per_owner, slots)

        @pl.when(high >= 0)
        def _():
            for place, local in ((0, low), (1, high)):
                grad_a[local] += terms[group, place, :, 0:width].astype(F32)
                grad_b[local] += terms[group, place, :, width:width + units].astype(F32)


def call(kernel, outs, specs):
    return pl.pallas_call(
        kernel,
        out_shape=outs,
        in_specs=specs,
        out_specs=jax.tree.map(lambda _: VMEM, outs),
        compiler_params=pltpu.CompilerParams(vmem_limit_bytes=LIMIT),
    )


def hop(value, axis, step):
    n = lax.axis_size(axis)
    return lax.ppermute(value, axis, [(i, (i + step) % n) for i in range(n)])


def on_device(tokens, cotangent, weight, down, up, used, order):
    n_y, n_z = lax.axis_size("y"), lax.axis_size("z")
    owners = lax.axis_size(DP)
    members = n_y * n_z
    rows, width = tokens.shape
    units = weight.shape[1]
    per_owner, _, rank = down.shape
    packed = -(-(width + units) // 128) * 128
    me = lax.axis_index(DP)
    whole = jax.ShapeDtypeStruct

    wide_tokens = lax.all_gather(tokens, "z", axis=1, tiled=True)

    weight_t = weight.T
    piece = n_y * width
    mine = lax.dynamic_slice(weight_t, (0, me * piece), (units, piece))
    spot = lax.axis_index("y")
    pieces = [
        hop(lax.dynamic_slice(mine, (0, lax.rem(spot + n_y - r, n_y) * width), (units, width)), "y", -r)
        if r else lax.dynamic_slice(mine, (0, spot * width), (units, width))
        for r in range(n_y)
    ]
    wide_weight = lax.all_gather(jnp.stack(pieces), DP, axis=2, tiled=True)

    down_t = jnp.transpose(down, (0, 2, 1))
    used_all = lax.all_to_all(
        jnp.broadcast_to(used[None], (owners,) + used.shape), DP, 0, 0, tiled=True
    ).reshape(owners, used.shape[1])
    me_arr = me.reshape(1).astype(jnp.int32)
    picked = call(pick_kernel, whole((owners, 2, rank, packed), BF), [SMEM, SMEM, VMEM, VMEM])(
        me_arr, used_all, down_t, up
    )
    factors = lax.all_to_all(picked, DP, 0, 0, tiled=True).reshape(owners * 2, rank, packed)
    cot_t = cotangent.T
    sizes = dict(rank=rank, width=width, units=units)
    part = call(
        functools.partial(parts_kernel, **sizes),
        whole((rows, 2 * rank), BF),
        [SMEM, SMEM, VMEM, VMEM, VMEM],
    )(used, order, factors, tokens, cot_t)
    share = rows // members
    parts = lax.all_to_all(part.reshape(members, share, 2 * rank), MP, 0, 0, tiled=True)
    summed = jnp.sum(parts.astype(F32), axis=0).astype(BF)
    both = lax.all_to_all(
        jnp.broadcast_to(summed[None], (members,) + summed.shape), MP, 0, 0, tiled=True
    ).reshape(rows, 2 * rank)
    send, delta = call(
        functools.partial(grads_kernel, **sizes),
        (whole((owners * 2, rank, packed), BF), whole((units, rows), F32)),
        [SMEM, SMEM, VMEM, VMEM, VMEM, VMEM],
    )(used, order, factors, tokens, cot_t, both)
    terms = lax.all_to_all(send.reshape(owners, 2, rank, packed), DP, 0, 0, tiled=True)
    grad_a, grad_b = call(
        sum_kernel,
        (whole((per_owner, rank, width), F32), whole((per_owner, rank, units), F32)),
        [SMEM, SMEM, VMEM],
    )(me_arr, used_all, terms)

    def product(r):
        return lax.dot_general(
            wide_weight[r], wide_tokens, (((1,), (1,)), ((), ())), preferred_element_type=F32
        )

    half = units // 2
    far = product(2).astype(BF)
    far_up, far_down = hop(far[:half], "y", 1), hop(far[half:], "y", -1)
    near_up, near_down = product(1), product(n_y - 1)
    near_up = jnp.concatenate([near_up[:half] + far_up.astype(F32), near_up[half:]]).astype(BF)
    near_down = jnp.concatenate(
        [near_down[:half], near_down[half:] + far_down.astype(F32)]
    ).astype(BF)
    got_up, got_down = hop(near_up, "y", 1), hop(near_down, "y", -1)
    out = product(0) + delta + got_up.astype(F32) + got_down.astype(F32)
    return out.astype(BF).T, jnp.transpose(grad_a, (0, 2, 1)), grad_b


def solution(mesh):
    grid = Mesh(mesh.devices.reshape(4, 2, 8, 4), ("x", "core", "z", "y"))
    return jax.shard_map(
        on_device,
        mesh=grid,
        in_specs=(
            P(DP, MP),
            P(DP, MP),
            P(None, MP),
            P(DP, MP, None),
            P(DP, None, MP),
            P(DP, None),
            P(DP, None),
        ),
        out_specs=(P(DP, MP), P(DP, MP, None), P(DP, None, MP)),
        check_vma=False,
    )
```

```python
import functools

import jax
import jax.numpy as jnp
from jax import lax
from jax.experimental import pallas as pl
from jax.experimental.pallas import tpu as pltpu
from jax.sharding import Mesh, PartitionSpec as P

BF = jnp.bfloat16
F32 = jnp.float32
DP = ("x", "core")
MP = ("z", "y")
VMEM = pl.BlockSpec(memory_space=pltpu.VMEM)
SMEM = pl.BlockSpec(memory_space=pltpu.SMEM)
LIMIT = 40 * 1024 * 1024


def pair_of(used, group, owner, per_owner, slots):
    low, high = jnp.int32(per_owner), jnp.int32(-1)
    for slot in range(slots):
        local = used[group, slot] - owner * per_owner
        inside = jnp.logical_and(local >= 0, local < per_owner)
        low = jnp.where(inside, jnp.minimum(low, local), low)
        high = jnp.where(inside, jnp.maximum(high, local), high)
    return low, high


def place_of(used, order, sequence, per_owner, slots):
    adapter = used[0, order[0, sequence]]
    owner = lax.div(adapter, jnp.int32(per_owner))
    second = jnp.int32(0)
    for slot in range(slots):
        other = used[0, slot]
        same = jnp.logical_and(lax.div(other, jnp.int32(per_owner)) == owner, other < adapter)
        second = jnp.where(same, jnp.int32(1), second)
    return owner * 2 + second


def pick_kernel(me, used, down, up, out):
    groups, slots = used.shape
    per_owner, rank, width = down.shape
    units = up.shape[2]
    for group in range(groups):
        low, high = pair_of(used, group, me[0], per_owner, slots)
        for place, local in ((0, low), (1, high)):
            index = jnp.clip(local, 0, per_owner - 1)
            out[group, place, :, 0:width] = down[index]
            out[group, place, :, width:width + units] = up[index]
            out[group, place, :, width + units:] = jnp.zeros((rank, out.shape[3] - width - units), BF)


def parts_kernel(used, order, factors, tokens, cot, out, *, rank, width, units):
    sequences = order.shape[1]
    length = tokens.shape[0] // sequences
    per_owner = sequences
    for i in range(sequences):
        place = place_of(used, order, i, per_owner, used.shape[1])
        own = factors[place]
        rows = tokens[i * length:(i + 1) * length, :]
        inputs = lax.dot_general(
            own[:, 0:width], rows, (((1,), (1,)), ((), ())), preferred_element_type=F32
        )
        back = 2.0 * jnp.dot(
            own[:, width:width + units],
            cot[:, i * length:(i + 1) * length],
            preferred_element_type=F32,
        )
        both = jnp.concatenate([inputs, back], axis=0)
        out[i * length:(i + 1) * length, :] = both.T.astype(BF)


def grads_kernel(used, order, factors, tokens, cot, both, send, delta, *, rank, width, units):
    sequences = order.shape[1]
    length = tokens.shape[0] // sequences
    per_owner = sequences
    send[...] = jnp.zeros(send.shape, BF)
    for i in range(sequences):
        place = place_of(used, order, i, per_owner, used.shape[1])
        span = slice(i * length, (i + 1) * length)
        turned = both[span, :].astype(F32).T.astype(BF)
        inputs, back = turned[0:rank, :], turned[rank:2 * rank, :]
        term_a = jnp.dot(back, tokens[span, :], preferred_element_type=F32)
        term_b = 2.0 * lax.dot_general(
            inputs, cot[:, span], (((1,), (1,)), ((), ())), preferred_element_type=F32
        )
        send[place, :, 0:width] = term_a.astype(BF)
        send[place, :, width:width + units] = term_b.astype(BF)
        up = factors[place][:, width:width + units]
        delta[:, span] = 2.0 * lax.dot_general(
            up, inputs, (((0,), (0,)), ((), ())), preferred_element_type=F32
        )


def sum_kernel(me, used, terms, grad_a, grad_b):
    groups, slots = used.shape
    per_owner, rank, width = grad_a.shape
    units = grad_b.shape[2]
    grad_a[...] = jnp.zeros(grad_a.shape, F32)
    grad_b[...] = jnp.zeros(grad_b.shape, F32)
    for group in range(groups):
        low, high = pair_of(used, group, me[0], per_owner, slots)

        @pl.when(high >= 0)
        def _():
            for place, local in ((0, low), (1, high)):
                grad_a[local] += terms[group, place, :, 0:width].astype(F32)
                grad_b[local] += terms[group, place, :, width:width + units].astype(F32)


def place_kernel(me, *refs):
    out = refs[-1]
    width = refs[0].shape[2]
    mid = refs[0].shape[0] // 2
    x, core = lax.div(me[0], jnp.int32(2)), lax.rem(me[0], jnp.int32(2))
    for other in range(2):
        for piece, step, start in ((0, 0, 0), (1, 3, 0), (2, 1, 0), (3, 2, 0), (4, 2, mid)):
            source = refs[5 * other + piece]
            block = 2 * lax.rem(x + step, jnp.int32(4)) + (1 - core if other else core)
            spot = pl.ds(pl.multiple_of(block * width, width), width)
            out[start:start + source.shape[0], :, spot] = source[...]


def call(kernel, outs, specs):
    return pl.pallas_call(
        kernel,
        out_shape=outs,
        in_specs=specs,
        out_specs=jax.tree.map(lambda _: VMEM, outs),
        compiler_params=pltpu.CompilerParams(vmem_limit_bytes=LIMIT),
    )


def hop(value, axis, step):
    n = lax.axis_size(axis)
    return lax.ppermute(value, axis, [(i, (i + step) % n) for i in range(n)])


def on_device(tokens, cotangent, weight, down, up, used, order):
    n_y, n_z = lax.axis_size("y"), lax.axis_size("z")
    owners = lax.axis_size(DP)
    members = n_y * n_z
    rows, width = tokens.shape
    units = weight.shape[1]
    per_owner, _, rank = down.shape
    packed = -(-(width + units) // 128) * 128
    me = lax.axis_index(DP)
    whole = jax.ShapeDtypeStruct

    wide_tokens = lax.all_gather(tokens, "z", axis=1, tiled=True)

    weight_t = weight.T
    piece = n_y * width
    mine = lax.dynamic_slice(weight_t, (0, me * piece), (units, piece))
    spot = lax.axis_index("y")
    pieces = [
        hop(lax.dynamic_slice(mine, (0, lax.rem(spot + n_y - r, n_y) * width), (units, width)), "y", -r)
        if r else lax.dynamic_slice(mine, (0, spot * width), (units, width))
        for r in range(n_y)
    ]
    own = jnp.stack(pieces)
    from_left, from_right = hop(own, "x", 1), hop(own, "x", -1)
    mid = n_y // 2
    far_left, far_right = hop(from_left[:mid], "x", 1), hop(from_right[mid:], "x", -1)
    held = (own, from_left, from_right, far_left, far_right)
    swapped = tuple(hop(piece, "core", 1) for piece in held)
    me_arr = me.reshape(1).astype(jnp.int32)
    wide_weight = call(
        place_kernel, whole((n_y, units, n_z * width), BF), [SMEM] + [VMEM] * 10
    )(me_arr, *held, *swapped)

    down_t = jnp.transpose(down, (0, 2, 1))
    used_all = lax.all_to_all(
        jnp.broadcast_to(used[None], (owners,) + used.shape), DP, 0, 0, tiled=True
    ).reshape(owners, used.shape[1])
    picked = call(pick_kernel, whole((owners, 2, rank, packed), BF), [SMEM, SMEM, VMEM, VMEM])(
        me_arr, used_all, down_t, up
    )
    factors = lax.all_to_all(picked, DP, 0, 0, tiled=True).reshape(owners * 2, rank, packed)
    cot_t = cotangent.T
    sizes = dict(rank=rank, width=width, units=units)
    part = call(
        functools.partial(parts_kernel, **sizes),
        whole((rows, 2 * rank), BF),
        [SMEM, SMEM, VMEM, VMEM, VMEM],
    )(used, order, factors, tokens, cot_t)
    share = rows // members
    parts = lax.all_to_all(part.reshape(members, share, 2 * rank), MP, 0, 0, tiled=True)
    summed = jnp.sum(parts.astype(F32), axis=0).astype(BF)
    both = lax.all_to_all(
        jnp.broadcast_to(summed[None], (members,) + summed.shape), MP, 0, 0, tiled=True
    ).reshape(rows, 2 * rank)
    send, delta = call(
        functools.partial(grads_kernel, **sizes),
        (whole((owners * 2, rank, packed), BF), whole((units, rows), F32)),
        [SMEM, SMEM, VMEM, VMEM, VMEM, VMEM],
    )(used, order, factors, tokens, cot_t, both)
    terms = lax.all_to_all(send.reshape(owners, 2, rank, packed), DP, 0, 0, tiled=True)
    grad_a, grad_b = call(
        sum_kernel,
        (whole((per_owner, rank, width), F32), whole((per_owner, rank, units), F32)),
        [SMEM, SMEM, VMEM],
    )(me_arr, used_all, terms)

    def product(r):
        return lax.dot_general(
            wide_weight[r], wide_tokens, (((1,), (1,)), ((), ())), preferred_element_type=F32
        )

    half = units // 2
    far = product(2).astype(BF)
    far_up, far_down = hop(far[:half], "y", 1), hop(far[half:], "y", -1)
    near_up, near_down = product(1), product(n_y - 1)
    near_up = jnp.concatenate([near_up[:half] + far_up.astype(F32), near_up[half:]]).astype(BF)
    near_down = jnp.concatenate(
        [near_down[:half], near_down[half:] + far_down.astype(F32)]
    ).astype(BF)
    got_up, got_down = hop(near_up, "y", 1), hop(near_down, "y", -1)
    out = product(0) + delta + got_up.astype(F32) + got_down.astype(F32)
    return out.astype(BF).T, jnp.transpose(grad_a, (0, 2, 1)), grad_b


def solution(mesh):
    grid = Mesh(mesh.devices.reshape(4, 2, 8, 4), ("x", "core", "z", "y"))
    return jax.shard_map(
        on_device,
        mesh=grid,
        in_specs=(
            P(DP, MP),
            P(DP, MP),
            P(None, MP),
            P(DP, MP, None),
            P(DP, None, MP),
            P(DP, None),
            P(DP, None),
        ),
        out_specs=(P(DP, MP), P(DP, MP, None), P(DP, None, MP)),
        check_vma=False,
    )
```

```python
import functools

import jax
import jax.numpy as jnp
from jax import lax
from jax.experimental import pallas as pl
from jax.experimental.pallas import tpu as pltpu
from jax.sharding import Mesh, PartitionSpec as P

BF = jnp.bfloat16
F32 = jnp.float32
DP = ("x", "core")
MP = ("z", "y")
VMEM = pl.BlockSpec(memory_space=pltpu.VMEM)
SMEM = pl.BlockSpec(memory_space=pltpu.SMEM)


def pair_of(used, group, owner, per_owner, slots):
    low, high = jnp.int32(per_owner), jnp.int32(-1)
    for slot in range(slots):
        local = used[group, slot] - owner * per_owner
        inside = jnp.logical_and(local >= 0, local < per_owner)
        low = jnp.where(inside, jnp.minimum(low, local), low)
        high = jnp.where(inside, jnp.maximum(high, local), high)
    return low, high


def place_of(used, order, sequence, per_owner, slots):
    adapter = used[0, order[0, sequence]]
    owner = lax.div(adapter, jnp.int32(per_owner))
    second = jnp.int32(0)
    for slot in range(slots):
        other = used[0, slot]
        same = jnp.logical_and(lax.div(other, jnp.int32(per_owner)) == owner, other < adapter)
        second = jnp.where(same, jnp.int32(1), second)
    return owner * 2 + second


def pick_kernel(me, used, down, up, out):
    groups, slots = used.shape
    per_owner, rank, width = down.shape
    units = up.shape[2]
    for group in range(groups):
        low, high = pair_of(used, group, me[0], per_owner, slots)
        for place, local in ((0, low), (1, high)):
            index = jnp.clip(local, 0, per_owner - 1)
            out[group, place, :, 0:width] = down[index]
            out[group, place, :, width:width + units] = up[index]
            out[group, place, :, width + units:] = jnp.zeros((rank, out.shape[3] - width - units), BF)


def parts_kernel(used, order, factors, tokens, cot, out, *, rank, width, units):
    sequences = order.shape[1]
    length = tokens.shape[0] // sequences
    per_owner = sequences
    for i in range(sequences):
        place = place_of(used, order, i, per_owner, used.shape[1])
        own = factors[place]
        rows = tokens[i * length:(i + 1) * length, :]
        inputs = lax.dot_general(
            own[:, 0:width], rows, (((1,), (1,)), ((), ())), preferred_element_type=F32
        )
        back = 2.0 * jnp.dot(
            own[:, width:width + units],
            cot[:, i * length:(i + 1) * length],
            preferred_element_type=F32,
        )
        both = jnp.concatenate([inputs, back], axis=0)
        out[i * length:(i + 1) * length, :] = both.T.astype(BF)


def grads_kernel(used, order, factors, tokens, cot, both, send, delta, *, rank, width, units):
    sequences = order.shape[1]
    length = tokens.shape[0] // sequences
    per_owner = sequences
    send[...] = jnp.zeros(send.shape, BF)
    for i in range(sequences):
        place = place_of(used, order, i, per_owner, used.shape[1])
        span = slice(i * length, (i + 1) * length)
        turned = both[span, :].astype(F32).T.astype(BF)
        inputs, back = turned[0:rank, :], turned[rank:2 * rank, :]
        term_a = jnp.dot(back, tokens[span, :], preferred_element_type=F32)
        term_b = 2.0 * lax.dot_general(
            inputs, cot[:, span], (((1,), (1,)), ((), ())), preferred_element_type=F32
        )
        send[place, :, 0:width] = term_a.astype(BF)
        send[place, :, width:width + units] = term_b.astype(BF)
        up = factors[place][:, width:width + units]
        delta[:, span] = 2.0 * lax.dot_general(
            up, inputs, (((0,), (0,)), ((), ())), preferred_element_type=F32
        )


def sum_kernel(me, used, terms, grad_a, grad_b):
    groups, slots = used.shape
    per_owner, rank, width = grad_a.shape
    units = grad_b.shape[2]
    grad_a[...] = jnp.zeros(grad_a.shape, F32)
    grad_b[...] = jnp.zeros(grad_b.shape, F32)
    for group in range(groups):
        low, high = pair_of(used, group, me[0], per_owner, slots)

        @pl.when(high >= 0)
        def _():
            for place, local in ((0, low), (1, high)):
                grad_a[local] += terms[group, place, :, 0:width].astype(F32)
                grad_b[local] += terms[group, place, :, width:width + units].astype(F32)


def gather_rows(meta, r, weights, tokens, wide, rows):
    width = tokens[0].shape[1]
    x, core, z = meta[0], meta[1], meta[2]
    mid = weights[0].shape[0] // 2
    for other in range(2):
        own, left, right, far_left, far_right = weights[5 * other:5 * other + 5]
        far = far_left.at[r] if r < mid else far_right.at[r - mid]
        for source, step in ((own.at[r], 0), (left.at[r], 3), (right.at[r], 1), (far, 2)):
            block = 2 * lax.rem(x + step, jnp.int32(4)) + (1 - core if other else core)
            place = lax.rem(block - z + 8, jnp.int32(8))
            wide[:, pl.ds(pl.multiple_of(place * width, width), width)] = source[...]
    if rows is not None:
        half = tokens[7].shape[0]
        own, f1, b1, f2, b2, f3, b3, f4, b4 = tokens
        for place, source in ((0, own), (1, b1), (2, b2), (3, b3), (5, f3), (6, f2), (7, f1)):
            rows[:, place * width:(place + 1) * width] = source[...]
        rows[0:half, 4 * width:5 * width] = f4[...]
        rows[half:2 * half, 4 * width:5 * width] = b4[...]


def multiply(wide, rows, store):
    step = 256

    @pl.loop(0, rows.shape[0] // step)
    def _(i):
        span = pl.ds(pl.multiple_of(i * step, step), step)
        store(span, lax.dot_general(
            wide[...], rows[span, :], (((1,), (1,)), ((), ())), preferred_element_type=F32
        ))


def far_kernel(meta, *refs):
    weights, tokens = refs[:10], refs[10:19]
    up, down, wide, rows = refs[19:]
    gather_rows(meta, 2, weights, tokens, wide, rows)
    half = up.shape[0]

    def store(span, value):
        up[:, span] = value[:half].astype(BF)
        down[:, span] = value[half:].astype(BF)

    multiply(wide, rows, store)


def near_kernel(meta, *refs):
    weights, tokens = refs[:10], refs[10:19]
    up_late, up_soon, down_soon, down_late, wide, rows = refs[19:]
    half = up_late.shape[0]
    gather_rows(meta, 1, weights, tokens, wide, rows)

    def store_up(span, value):
        up_late[:, span] = value[:half]
        up_soon[:, span] = value[half:].astype(BF)

    multiply(wide, rows, store_up)
    gather_rows(meta, 3, weights, tokens, wide, None)

    def store_down(span, value):
        down_soon[:, span] = value[:half].astype(BF)
        down_late[:, span] = value[half:]

    multiply(wide, rows, store_down)


def own_kernel(meta, *refs):
    weights, tokens = refs[:10], refs[10:19]
    delta, out, wide, rows = refs[19:]
    gather_rows(meta, 0, weights, tokens, wide, rows)

    def store(span, value):
        out[:, span] = value + delta[:, span]

    multiply(wide, rows, store)


def join_kernel(base, up_late, up_soon, down_soon, down_late, out):
    half = up_late.shape[0]
    out[0:half, :] = (
        base[0:half, :] + up_late[...].astype(F32) + down_soon[...].astype(F32)
    ).astype(BF)
    out[half:, :] = (
        base[half:, :] + up_soon[...].astype(F32) + down_late[...].astype(F32)
    ).astype(BF)


def call(kernel, outs, specs, scratch=(), limit=16):
    return pl.pallas_call(
        kernel,
        out_shape=outs,
        in_specs=specs,
        out_specs=jax.tree.map(lambda _: VMEM, outs),
        scratch_shapes=scratch,
        compiler_params=pltpu.CompilerParams(vmem_limit_bytes=limit * 1024 * 1024),
    )


def hop(value, axis, step):
    n = lax.axis_size(axis)
    return lax.ppermute(value, axis, [(i, (i + step) % n) for i in range(n)])


def on_device(tokens, cotangent, weight, down, up, used, order):
    n_y, n_z = lax.axis_size("y"), lax.axis_size("z")
    owners = lax.axis_size(DP)
    members = n_y * n_z
    rows, width = tokens.shape
    units = weight.shape[1]
    per_owner, _, rank = down.shape
    packed = -(-(width + units) // 128) * 128
    me = lax.axis_index(DP)
    whole = jax.ShapeDtypeStruct

    together = lax.optimization_barrier
    x, core, z, y = (lax.axis_index(name) for name in ("x", "core", "z", "y"))
    meta = jnp.stack([x, core, z, y]).astype(jnp.int32)
    me_arr = me.reshape(1).astype(jnp.int32)

    weight_t = weight.T
    piece = n_y * width
    mine = lax.dynamic_slice(weight_t, (0, me * piece), (units, piece))
    pieces = [
        hop(lax.dynamic_slice(mine, (0, lax.rem(y + n_y - r, n_y) * width), (units, width)), "y", -r)
        if r else lax.dynamic_slice(mine, (0, y * width), (units, width))
        for r in range(n_y)
    ]
    f1, b1 = hop(tokens, "z", 1), hop(tokens, "z", -1)

    down_t = jnp.transpose(down, (0, 2, 1))
    used_all = lax.all_to_all(
        jnp.broadcast_to(used[None], (owners,) + used.shape), DP, 0, 0, tiled=True
    ).reshape(owners, used.shape[1])
    picked = call(pick_kernel, whole((owners, 2, rank, packed), BF), [SMEM, SMEM, VMEM, VMEM])(
        me_arr, used_all, down_t, up
    )
    picked, pieces, f1, b1 = together((picked, pieces, f1, b1))
    own = jnp.stack(pieces)
    from_left, from_right = hop(own, "x", 1), hop(own, "x", -1)
    f2, b2 = hop(f1, "z", 1), hop(b1, "z", -1)
    factors = lax.all_to_all(picked, DP, 0, 0, tiled=True).reshape(owners * 2, rank, packed)
    f3, b3 = hop(f2, "z", 1), hop(b2, "z", -1)
    cot_t = cotangent.T
    sizes = dict(rank=rank, width=width, units=units)
    part = call(
        functools.partial(parts_kernel, **sizes),
        whole((rows, 2 * rank), BF),
        [SMEM, SMEM, VMEM, VMEM, VMEM],
    )(used, order, factors, tokens, cot_t)
    part, from_left, from_right, f2, b2 = together((part, from_left, from_right, f2, b2))
    mid, halfway = n_y // 2, rows // 2
    far_left, far_right = hop(from_left[:mid], "x", 1), hop(from_right[mid:], "x", -1)
    f4, b4 = hop(f3[:halfway], "z", 1), hop(b3[halfway:], "z", -1)
    held = (own, from_left, from_right, far_left, far_right)
    swapped = tuple(hop(item, "core", 1) for item in held)
    share = rows // members
    parts = lax.all_to_all(part.reshape(members, share, 2 * rank), MP, 0, 0, tiled=True)
    summed = jnp.sum(parts.astype(F32), axis=0).astype(BF)
    both = lax.all_to_all(
        jnp.broadcast_to(summed[None], (members,) + summed.shape), MP, 0, 0, tiled=True
    ).reshape(rows, 2 * rank)

    blocks = (meta, *held, *swapped, tokens, f1, b1, f2, b2, f3, b3, f4, b4)
    specs = [SMEM] + [VMEM] * 19
    scratch = [pltpu.VMEM((units, n_z * width), BF), pltpu.VMEM((rows, n_z * width), BF)]
    half = units // 2
    narrow, broad = whole((half, rows), BF), whole((half, rows), F32)
    far_up, far_down = call(far_kernel, (narrow, narrow), specs, scratch, 32)(*blocks)
    far_up, far_down = hop(far_up, "y", 1), hop(far_down, "y", -1)
    up_late, up_soon, down_soon, down_late = call(
        near_kernel, (broad, narrow, narrow, broad), specs, scratch, 32
    )(*blocks)
    up_soon, down_soon = hop(up_soon, "y", 1), hop(down_soon, "y", -1)
    up_late = hop((up_late + far_up.astype(F32)).astype(BF), "y", 1)
    down_late = hop((down_late + far_down.astype(F32)).astype(BF), "y", -1)

    send, delta = call(
        functools.partial(grads_kernel, **sizes),
        (whole((owners * 2, rank, packed), BF), whole((units, rows), F32)),
        [SMEM, SMEM, VMEM, VMEM, VMEM, VMEM],
    )(used, order, factors, tokens, cot_t, both)
    terms = lax.all_to_all(send.reshape(owners, 2, rank, packed), DP, 0, 0, tiled=True)
    grad_a, grad_b = call(
        sum_kernel,
        (whole((per_owner, rank, width), F32), whole((per_owner, rank, units), F32)),
        [SMEM, SMEM, VMEM],
    )(me_arr, used_all, terms)

    base = call(own_kernel, whole((units, rows), F32), specs + [VMEM], scratch, 32)(*blocks, delta)
    out = call(join_kernel, whole((units, rows), BF), [VMEM] * 5)(
        base, up_late, up_soon, down_soon, down_late
    )
    return out.T, jnp.transpose(grad_a, (0, 2, 1)), grad_b


def solution(mesh):
    grid = Mesh(mesh.devices.reshape(4, 2, 8, 4), ("x", "core", "z", "y"))
    return jax.shard_map(
        on_device,
        mesh=grid,
        in_specs=(
            P(DP, MP),
            P(DP, MP),
            P(None, MP),
            P(DP, MP, None),
            P(DP, None, MP),
            P(DP, None),
            P(DP, None),
        ),
        out_specs=(P(DP, MP), P(DP, MP, None), P(DP, None, MP)),
        check_vma=False,
    )
```

```python
import functools

import jax
import jax.numpy as jnp
from jax import lax
from jax.experimental import pallas as pl
from jax.experimental.pallas import tpu as pltpu
from jax.sharding import Mesh, PartitionSpec as P

BF = jnp.bfloat16
F32 = jnp.float32
DP = ("x", "core")
MP = ("z", "y")
VMEM = pl.BlockSpec(memory_space=pltpu.VMEM)
SMEM = pl.BlockSpec(memory_space=pltpu.SMEM)


def pair_of(used, group, owner, per_owner, slots):
    low, high = jnp.int32(per_owner), jnp.int32(-1)
    for slot in range(slots):
        local = used[group, slot] - owner * per_owner
        inside = jnp.logical_and(local >= 0, local < per_owner)
        low = jnp.where(inside, jnp.minimum(low, local), low)
        high = jnp.where(inside, jnp.maximum(high, local), high)
    return low, high


def place_of(used, order, sequence, per_owner, slots):
    adapter = used[0, order[0, sequence]]
    owner = lax.div(adapter, jnp.int32(per_owner))
    second = jnp.int32(0)
    for slot in range(slots):
        other = used[0, slot]
        same = jnp.logical_and(lax.div(other, jnp.int32(per_owner)) == owner, other < adapter)
        second = jnp.where(same, jnp.int32(1), second)
    return owner * 2 + second


def pick_kernel(me, used, down, up, out):
    groups, slots = used.shape
    per_owner, rank, width = down.shape
    units = up.shape[2]
    for group in range(groups):
        low, high = pair_of(used, group, me[0], per_owner, slots)
        for place, local in ((0, low), (1, high)):
            index = jnp.clip(local, 0, per_owner - 1)
            out[group, place, :, 0:width] = down[index]
            out[group, place, :, width:width + units] = up[index]
            out[group, place, :, width + units:] = jnp.zeros((rank, out.shape[3] - width - units), BF)


def parts_kernel(used, order, factors, tokens, cot, out, *, rank, width, units):
    sequences = order.shape[1]
    length = tokens.shape[0] // sequences
    per_owner = sequences
    for i in range(sequences):
        place = place_of(used, order, i, per_owner, used.shape[1])
        own = factors[place]
        rows = tokens[i * length:(i + 1) * length, :]
        inputs = lax.dot_general(
            own[:, 0:width], rows, (((1,), (1,)), ((), ())), preferred_element_type=F32
        )
        back = 2.0 * jnp.dot(
            own[:, width:width + units],
            cot[:, i * length:(i + 1) * length],
            preferred_element_type=F32,
        )
        both = jnp.concatenate([inputs, back], axis=0)
        out[i * length:(i + 1) * length, :] = both.T.astype(BF)


def grads_kernel(used, order, factors, tokens, cot, both, send, delta, *, rank, width, units):
    sequences = order.shape[1]
    length = tokens.shape[0] // sequences
    per_owner = sequences
    send[...] = jnp.zeros(send.shape, BF)
    for i in range(sequences):
        place = place_of(used, order, i, per_owner, used.shape[1])
        span = slice(i * length, (i + 1) * length)
        turned = both[span, :].astype(F32).T.astype(BF)
        inputs, back = turned[0:rank, :], turned[rank:2 * rank, :]
        term_a = jnp.dot(back, tokens[span, :], preferred_element_type=F32)
        term_b = 2.0 * lax.dot_general(
            inputs, cot[:, span], (((1,), (1,)), ((), ())), preferred_element_type=F32
        )
        send[place, :, 0:width] = term_a.astype(BF)
        send[place, :, width:width + units] = term_b.astype(BF)
        up = factors[place][:, width:width + units]
        delta[:, span] = 2.0 * lax.dot_general(
            up, inputs, (((0,), (0,)), ((), ())), preferred_element_type=F32
        )


def sum_kernel(me, used, terms, grad_a, grad_b):
    groups, slots = used.shape
    per_owner, rank, width = grad_a.shape
    units = grad_b.shape[2]
    grad_a[...] = jnp.zeros(grad_a.shape, F32)
    grad_b[...] = jnp.zeros(grad_b.shape, F32)
    for group in range(groups):
        low, high = pair_of(used, group, me[0], per_owner, slots)

        @pl.when(high >= 0)
        def _():
            for place, local in ((0, low), (1, high)):
                grad_a[local] += terms[group, place, :, 0:width].astype(F32)
                grad_b[local] += terms[group, place, :, width:width + units].astype(F32)


def place_kernel(meta, *refs):
    out = refs[-1]
    count, units, _ = out.shape
    width = refs[0].shape[1]
    half = refs[3].shape[0]
    x, core = meta[0], meta[1]
    for other in range(2):
        own, left, right, far_left, far_right = refs[5 * other:5 * other + 5]
        for sources, step in (((own,), 0), ((left,), 3), ((right,), 1), ((far_left, far_right), 2)):
            block = 2 * lax.rem(x + step, jnp.int32(4)) + (1 - core if other else core)
            spot = pl.ds(pl.multiple_of(block * width, width), width)
            for r in range(count):
                for start in range(0, units, units // 2):
                    at = r * units + start
                    source = sources[at // half] if len(sources) == 2 else sources[0]
                    low = at % half if len(sources) == 2 else at
                    out[r, start:start + units // 2, spot] = source[low:low + units // 2, :]


def copy_kernel(meta, source, out):
    out[...] = source[...]


def join_kernel(base, up_late, up_soon, down_soon, down_late, out):
    half = up_late.shape[0]
    out[0:half, :] = (
        base[0:half, :] + up_late[...].astype(F32) + down_soon[...].astype(F32)
    ).astype(BF)
    out[half:, :] = (
        base[half:, :] + up_soon[...].astype(F32) + down_late[...].astype(F32)
    ).astype(BF)


def call(kernel, outs, specs, scratch=(), limit=16):
    return pl.pallas_call(
        kernel,
        out_shape=outs,
        in_specs=specs,
        out_specs=jax.tree.map(lambda _: VMEM, outs),
        scratch_shapes=scratch,
        compiler_params=pltpu.CompilerParams(vmem_limit_bytes=limit * 1024 * 1024),
    )


def hop(value, axis, step):
    n = lax.axis_size(axis)
    return lax.ppermute(value, axis, [(i, (i + step) % n) for i in range(n)])


def on_device(tokens, cotangent, weight, down, up, used, order):
    n_y, n_z = lax.axis_size("y"), lax.axis_size("z")
    owners = lax.axis_size(DP)
    members = n_y * n_z
    rows, width = tokens.shape
    units = weight.shape[1]
    per_owner, _, rank = down.shape
    packed = -(-(width + units) // 128) * 128
    me = lax.axis_index(DP)
    whole = jax.ShapeDtypeStruct

    together = lax.optimization_barrier
    x, core, z, y = (lax.axis_index(name) for name in ("x", "core", "z", "y"))
    meta = jnp.stack([x, core, z, y]).astype(jnp.int32)
    me_arr = me.reshape(1).astype(jnp.int32)

    wide_tokens = lax.all_gather(tokens, "z", axis=1, tiled=True)

    weight_t = weight.T
    piece = n_y * width
    mine = lax.dynamic_slice(weight_t, (0, me * piece), (units, piece))
    pieces = tuple(
        hop(lax.dynamic_slice(mine, (0, lax.rem(y + n_y - r, n_y) * width), (units, width)), "y", -r)
        for r in range(1, n_y)
    )

    down_t = jnp.transpose(down, (0, 2, 1))
    used_all = lax.all_to_all(
        jnp.broadcast_to(used[None], (owners,) + used.shape), DP, 0, 0, tiled=True
    ).reshape(owners, used.shape[1])
    picked = call(pick_kernel, whole((owners, 2, rank, packed), BF), [SMEM, SMEM, VMEM, VMEM])(
        me_arr, used_all, down_t, up
    )
    picked, pieces = together((picked, pieces))
    own = jnp.concatenate(pieces, axis=0)
    from_left, from_right = hop(own, "x", 1), hop(own, "x", -1)
    factors = lax.all_to_all(picked, DP, 0, 0, tiled=True).reshape(owners * 2, rank, packed)
    cot_t = cotangent.T
    sizes = dict(rank=rank, width=width, units=units)
    part = call(
        functools.partial(parts_kernel, **sizes),
        whole((rows, 2 * rank), BF),
        [SMEM, SMEM, VMEM, VMEM, VMEM],
    )(used, order, factors, tokens, cot_t)
    part, weight_t = together((part, weight_t))
    own_weight = pl.pallas_call(
        copy_kernel,
        out_shape=whole((units, n_z * width), BF),
        grid_spec=pltpu.PrefetchScalarGridSpec(
            num_scalar_prefetch=1,
            grid=(n_z,),
            in_specs=[pl.BlockSpec((units, width), lambda i, meta: (0, i * n_y + meta[3]))],
            out_specs=pl.BlockSpec((units, width), lambda i, meta: (0, i)),
        ),
    )(meta, weight_t)
    middle = own.shape[0] // 2
    far_left, far_right = hop(from_left[:middle], "x", 1), hop(from_right[middle:], "x", -1)
    held = (own, from_left, from_right, far_left, far_right)
    swapped = tuple(hop(item, "core", 1) for item in held)
    wide_weight = call(
        place_kernel, whole((n_y - 1, units, n_z * width), BF), [SMEM] + [VMEM] * 10, limit=24
    )(meta, *held, *swapped)
    share = rows // members
    parts = lax.all_to_all(part.reshape(members, share, 2 * rank), MP, 0, 0, tiled=True)
    summed = jnp.sum(parts.astype(F32), axis=0).astype(BF)
    both = lax.all_to_all(
        jnp.broadcast_to(summed[None], (members,) + summed.shape), MP, 0, 0, tiled=True
    ).reshape(rows, 2 * rank)

    half = units // 2

    def product(weights):
        return lax.dot_general(
            weights, wide_tokens, (((1,), (1,)), ((), ())), preferred_element_type=F32
        )

    near, far, back = (wide_weight[r] for r in range(3))
    far_up = hop(product(far[:half]).astype(BF), "y", 1)
    far_down = hop(product(far[half:]).astype(BF), "y", -1)
    up_soon = hop(product(near[half:]).astype(BF), "y", 1)
    down_soon = hop(product(back[:half]).astype(BF), "y", -1)
    up_late = hop((product(near[:half]) + far_up.astype(F32)).astype(BF), "y", 1)
    down_late = hop((product(back[half:]) + far_down.astype(F32)).astype(BF), "y", -1)

    send, delta = call(
        functools.partial(grads_kernel, **sizes),
        (whole((owners * 2, rank, packed), BF), whole((units, rows), F32)),
        [SMEM, SMEM, VMEM, VMEM, VMEM, VMEM],
    )(used, order, factors, tokens, cot_t, both)
    terms = lax.all_to_all(send.reshape(owners, 2, rank, packed), DP, 0, 0, tiled=True)
    grad_a, grad_b = call(
        sum_kernel,
        (whole((per_owner, rank, width), F32), whole((per_owner, rank, units), F32)),
        [SMEM, SMEM, VMEM],
    )(me_arr, used_all, terms)

    base = together(product(own_weight) + delta)
    out = call(join_kernel, whole((units, rows), BF), [VMEM] * 5)(
        base, up_late, up_soon, down_soon, down_late
    )
    return out.T, jnp.transpose(grad_a, (0, 2, 1)), grad_b


def solution(mesh):
    grid = Mesh(mesh.devices.reshape(4, 2, 8, 4), ("x", "core", "z", "y"))
    return jax.shard_map(
        on_device,
        mesh=grid,
        in_specs=(
            P(DP, MP),
            P(DP, MP),
            P(None, MP),
            P(DP, MP, None),
            P(DP, None, MP),
            P(DP, None),
            P(DP, None),
        ),
        out_specs=(P(DP, MP), P(DP, MP, None), P(DP, None, MP)),
        check_vma=False,
    )
```

```python
import functools

import jax
import jax.numpy as jnp
from jax import lax
from jax.experimental import pallas as pl
from jax.experimental.pallas import tpu as pltpu
from jax.sharding import Mesh, PartitionSpec as P

BF = jnp.bfloat16
F32 = jnp.float32
DP = ("x", "core")
MP = ("z", "y")
VMEM = pl.BlockSpec(memory_space=pltpu.VMEM)
SMEM = pl.BlockSpec(memory_space=pltpu.SMEM)


def pair_of(used, group, owner, per_owner, slots):
    low, high = jnp.int32(per_owner), jnp.int32(-1)
    for slot in range(slots):
        local = used[group, slot] - owner * per_owner
        inside = jnp.logical_and(local >= 0, local < per_owner)
        low = jnp.where(inside, jnp.minimum(low, local), low)
        high = jnp.where(inside, jnp.maximum(high, local), high)
    return low, high


def place_of(used, order, sequence, per_owner, slots):
    adapter = used[0, order[0, sequence]]
    owner = lax.div(adapter, jnp.int32(per_owner))
    second = jnp.int32(0)
    for slot in range(slots):
        other = used[0, slot]
        same = jnp.logical_and(lax.div(other, jnp.int32(per_owner)) == owner, other < adapter)
        second = jnp.where(same, jnp.int32(1), second)
    return owner * 2 + second


def pick_kernel(me, used, down, up, out):
    groups, slots = used.shape
    per_owner, rank, width = down.shape
    units = up.shape[2]
    for group in range(groups):
        low, high = pair_of(used, group, me[0], per_owner, slots)
        for place, local in ((0, low), (1, high)):
            index = jnp.clip(local, 0, per_owner - 1)
            out[group, place, :, 0:width] = down[index]
            out[group, place, :, width:width + units] = up[index]
            out[group, place, :, width + units:] = jnp.zeros((rank, out.shape[3] - width - units), BF)


def parts_kernel(used, order, factors, tokens, cot, out, *, rank, width, units):
    sequences = order.shape[1]
    length = tokens.shape[0] // sequences
    per_owner = sequences
    for i in range(sequences):
        place = place_of(used, order, i, per_owner, used.shape[1])
        own = factors[place]
        rows = tokens[i * length:(i + 1) * length, :]
        inputs = lax.dot_general(
            own[:, 0:width], rows, (((1,), (1,)), ((), ())), preferred_element_type=F32
        )
        back = 2.0 * jnp.dot(
            own[:, width:width + units],
            cot[:, i * length:(i + 1) * length],
            preferred_element_type=F32,
        )
        both = jnp.concatenate([inputs, back], axis=0)
        out[i * length:(i + 1) * length, :] = both.T.astype(BF)


def grads_kernel(used, order, factors, tokens, cot, both, send, delta, *, rank, width, units):
    sequences = order.shape[1]
    length = tokens.shape[0] // sequences
    per_owner = sequences
    send[...] = jnp.zeros(send.shape, BF)
    for i in range(sequences):
        place = place_of(used, order, i, per_owner, used.shape[1])
        span = slice(i * length, (i + 1) * length)
        turned = both[span, :].astype(F32).T.astype(BF)
        inputs, back = turned[0:rank, :], turned[rank:2 * rank, :]
        term_a = jnp.dot(back, tokens[span, :], preferred_element_type=F32)
        term_b = 2.0 * lax.dot_general(
            inputs, cot[:, span], (((1,), (1,)), ((), ())), preferred_element_type=F32
        )
        send[place, :, 0:width] = term_a.astype(BF)
        send[place, :, width:width + units] = term_b.astype(BF)
        up = factors[place][:, width:width + units]
        delta[:, span] = 2.0 * lax.dot_general(
            up, inputs, (((0,), (0,)), ((), ())), preferred_element_type=F32
        )


def sum_kernel(me, used, terms, grad_a, grad_b):
    groups, slots = used.shape
    per_owner, rank, width = grad_a.shape
    units = grad_b.shape[2]
    grad_a[...] = jnp.zeros(grad_a.shape, F32)
    grad_b[...] = jnp.zeros(grad_b.shape, F32)
    for group in range(groups):
        low, high = pair_of(used, group, me[0], per_owner, slots)

        @pl.when(high >= 0)
        def _():
            for place, local in ((0, low), (1, high)):
                grad_a[local] += terms[group, place, :, 0:width].astype(F32)
                grad_b[local] += terms[group, place, :, width:width + units].astype(F32)


def place_kernel(meta, *refs):
    got, swapped, out = refs[:3], refs[3:6], refs[6]
    span = got[0].shape[1]
    core = meta[1]
    for r in range(3):
        out[r, :, pl.ds(pl.multiple_of(core * span, span), span)] = got[r][...]
        out[r, :, pl.ds(pl.multiple_of((1 - core) * span, span), span)] = swapped[r][...]


def fetch_kernel(meta, *refs):
    for source, out in zip(refs[:3], refs[3:]):
        out[...] = source[...]


def join_blocks_kernel(source, out):
    out[...] = source[0]


def copy_kernel(meta, source, out):
    out[...] = source[...]


def join_kernel(base, up_late, up_soon, down_soon, down_late, out):
    half = up_late.shape[0]
    out[0:half, :] = (
        base[0:half, :] + up_late[...].astype(F32) + down_soon[...].astype(F32)
    ).astype(BF)
    out[half:, :] = (
        base[half:, :] + up_soon[...].astype(F32) + down_late[...].astype(F32)
    ).astype(BF)


def call(kernel, outs, specs, scratch=(), limit=16):
    return pl.pallas_call(
        kernel,
        out_shape=outs,
        in_specs=specs,
        out_specs=jax.tree.map(lambda _: VMEM, outs),
        scratch_shapes=scratch,
        compiler_params=pltpu.CompilerParams(vmem_limit_bytes=limit * 1024 * 1024),
    )


def hop(value, axis, step):
    n = lax.axis_size(axis)
    return lax.ppermute(value, axis, [(i, (i + step) % n) for i in range(n)])


def on_device(tokens, cotangent, weight, down, up, used, order):
    n_y, n_z = lax.axis_size("y"), lax.axis_size("z")
    owners = lax.axis_size(DP)
    members = n_y * n_z
    rows, width = tokens.shape
    units = weight.shape[1]
    per_owner, _, rank = down.shape
    packed = -(-(width + units) // 128) * 128
    me = lax.axis_index(DP)
    whole = jax.ShapeDtypeStruct

    together = lax.optimization_barrier
    x, core, z, y = (lax.axis_index(name) for name in ("x", "core", "z", "y"))
    meta = jnp.stack([x, core, z, y]).astype(jnp.int32)
    me_arr = me.reshape(1).astype(jnp.int32)

    gathered = lax.all_gather(tokens, "z")

    weight_t = weight.T
    span = n_z // 2

    def block_for(r):
        return lambda i, meta: (
            0, (span * meta[1] + i) * n_y + lax.rem(meta[3] + n_y - r, jnp.int32(n_y))
        )

    fetched = pl.pallas_call(
        fetch_kernel,
        out_shape=[whole((units, span * width), BF)] * 3,
        grid_spec=pltpu.PrefetchScalarGridSpec(
            num_scalar_prefetch=1,
            grid=(span,),
            in_specs=[pl.BlockSpec((units, width), block_for(r)) for r in (1, 2, 3)],
            out_specs=[pl.BlockSpec((units, width), lambda i, meta: (0, i))] * 3,
        ),
    )(meta, weight_t, weight_t, weight_t)
    pieces = tuple(hop(item, "y", -r) for r, item in zip((1, 2, 3), fetched))

    down_t = jnp.transpose(down, (0, 2, 1))
    used_all = lax.all_to_all(
        jnp.broadcast_to(used[None], (owners,) + used.shape), DP, 0, 0, tiled=True
    ).reshape(owners, used.shape[1])
    picked = call(pick_kernel, whole((owners, 2, rank, packed), BF), [SMEM, SMEM, VMEM, VMEM])(
        me_arr, used_all, down_t, up
    )
    factors = lax.all_to_all(picked, DP, 0, 0, tiled=True).reshape(owners * 2, rank, packed)
    cot_t = cotangent.T
    sizes = dict(rank=rank, width=width, units=units)
    part = call(
        functools.partial(parts_kernel, **sizes),
        whole((rows, 2 * rank), BF),
        [SMEM, SMEM, VMEM, VMEM, VMEM],
    )(used, order, factors, tokens, cot_t)
    part, weight_t = together((part, weight_t))
    own_weight = pl.pallas_call(
        copy_kernel,
        out_shape=whole((units, n_z * width), BF),
        grid_spec=pltpu.PrefetchScalarGridSpec(
            num_scalar_prefetch=1,
            grid=(n_z,),
            in_specs=[pl.BlockSpec((units, width), lambda i, meta: (0, i * n_y + meta[3]))],
            out_specs=pl.BlockSpec((units, width), lambda i, meta: (0, i)),
        ),
    )(meta, weight_t)
    swapped = tuple(hop(item, "core", 1) for item in pieces)
    wide_weight = call(
        place_kernel, whole((n_y - 1, units, n_z * width), BF), [SMEM] + [VMEM] * 6, limit=24
    )(meta, *pieces, *swapped)
    share = rows // members
    parts = lax.all_to_all(part.reshape(members, share, 2 * rank), MP, 0, 0, tiled=True)
    summed = jnp.sum(parts.astype(F32), axis=0).astype(BF)
    both = lax.all_to_all(
        jnp.broadcast_to(summed[None], (members,) + summed.shape), MP, 0, 0, tiled=True
    ).reshape(rows, 2 * rank)

    wide_tokens = pl.pallas_call(
        join_blocks_kernel,
        out_shape=whole((rows, n_z * width), BF),
        grid=(n_z,),
        in_specs=[pl.BlockSpec((1, rows, width), lambda i: (i, 0, 0))],
        out_specs=pl.BlockSpec((rows, width), lambda i: (0, i)),
    )(gathered)
    half = units // 2

    def product(weights):
        return lax.dot_general(
            weights, wide_tokens, (((1,), (1,)), ((), ())), preferred_element_type=F32
        )

    near, far, back = (wide_weight[r] for r in range(3))
    far_up = hop(product(far[:half]).astype(BF), "y", 1)
    far_down = hop(product(far[half:]).astype(BF), "y", -1)
    up_soon = hop(product(near[half:]).astype(BF), "y", 1)
    down_soon = hop(product(back[:half]).astype(BF), "y", -1)
    up_late = hop((product(near[:half]) + far_up.astype(F32)).astype(BF), "y", 1)
    down_late = hop((product(back[half:]) + far_down.astype(F32)).astype(BF), "y", -1)

    send, delta = call(
        functools.partial(grads_kernel, **sizes),
        (whole((owners * 2, rank, packed), BF), whole((units, rows), F32)),
        [SMEM, SMEM, VMEM, VMEM, VMEM, VMEM],
    )(used, order, factors, tokens, cot_t, both)
    terms = lax.all_to_all(send.reshape(owners, 2, rank, packed), DP, 0, 0, tiled=True)
    grad_a, grad_b = call(
        sum_kernel,
        (whole((per_owner, rank, width), F32), whole((per_owner, rank, units), F32)),
        [SMEM, SMEM, VMEM],
    )(me_arr, used_all, terms)

    base = together(product(own_weight) + delta)
    out = call(join_kernel, whole((units, rows), BF), [VMEM] * 5)(
        base, up_late, up_soon, down_soon, down_late
    )
    return out.T, jnp.transpose(grad_a, (0, 2, 1)), grad_b


def solution(mesh):
    grid = Mesh(mesh.devices.reshape(4, 2, 8, 4), ("x", "core", "z", "y"))
    return jax.shard_map(
        on_device,
        mesh=grid,
        in_specs=(
            P(DP, MP),
            P(DP, MP),
            P(None, MP),
            P(DP, MP, None),
            P(DP, None, MP),
            P(DP, None),
            P(DP, None),
        ),
        out_specs=(P(DP, MP), P(DP, MP, None), P(DP, None, MP)),
        check_vma=False,
    )
```

```python
import functools

import jax
import jax.numpy as jnp
from jax import lax
from jax.experimental import pallas as pl
from jax.experimental.pallas import tpu as pltpu
from jax.sharding import Mesh, PartitionSpec as P

BF = jnp.bfloat16
F32 = jnp.float32
DP = ("x", "core")
MP = ("z", "y")
VMEM = pl.BlockSpec(memory_space=pltpu.VMEM)
SMEM = pl.BlockSpec(memory_space=pltpu.SMEM)


def pair_of(used, group, owner, per_owner, slots):
    low, high = jnp.int32(per_owner), jnp.int32(-1)
    for slot in range(slots):
        local = used[group, slot] - owner * per_owner
        inside = jnp.logical_and(local >= 0, local < per_owner)
        low = jnp.where(inside, jnp.minimum(low, local), low)
        high = jnp.where(inside, jnp.maximum(high, local), high)
    return low, high


def place_of(used, order, sequence, per_owner, slots):
    adapter = used[0, order[0, sequence]]
    owner = lax.div(adapter, jnp.int32(per_owner))
    second = jnp.int32(0)
    for slot in range(slots):
        other = used[0, slot]
        same = jnp.logical_and(lax.div(other, jnp.int32(per_owner)) == owner, other < adapter)
        second = jnp.where(same, jnp.int32(1), second)
    return owner * 2 + second


def pick_kernel(me, used, down, up, out):
    groups, slots = used.shape
    per_owner, rank, width = down.shape
    units = up.shape[2]
    for group in range(groups):
        low, high = pair_of(used, group, me[0], per_owner, slots)
        for place, local in ((0, low), (1, high)):
            index = jnp.clip(local, 0, per_owner - 1)
            out[group, place, :, 0:width] = down[index]
            out[group, place, :, width:width + units] = up[index]
            out[group, place, :, width + units:] = jnp.zeros((rank, out.shape[3] - width - units), BF)


def parts_kernel(used, order, factors, tokens, cot, out, *, rank, width, units):
    sequences = order.shape[1]
    length = tokens.shape[0] // sequences
    per_owner = sequences
    for i in range(sequences):
        place = place_of(used, order, i, per_owner, used.shape[1])
        own = factors[place]
        rows = tokens[i * length:(i + 1) * length, :]
        inputs = lax.dot_general(
            own[:, 0:width], rows, (((1,), (1,)), ((), ())), preferred_element_type=F32
        )
        back = 2.0 * jnp.dot(
            own[:, width:width + units],
            cot[:, i * length:(i + 1) * length],
            preferred_element_type=F32,
        )
        both = jnp.concatenate([inputs, back], axis=0)
        out[i * length:(i + 1) * length, :] = both.T.astype(BF)


def grads_kernel(used, order, factors, tokens, cot, both, send, delta, *, rank, width, units):
    sequences = order.shape[1]
    length = tokens.shape[0] // sequences
    per_owner = sequences
    send[...] = jnp.zeros(send.shape, BF)
    for i in range(sequences):
        place = place_of(used, order, i, per_owner, used.shape[1])
        span = slice(i * length, (i + 1) * length)
        turned = both[span, :].astype(F32).T.astype(BF)
        inputs, back = turned[0:rank, :], turned[rank:2 * rank, :]
        term_a = jnp.dot(back, tokens[span, :], preferred_element_type=F32)
        term_b = 2.0 * lax.dot_general(
            inputs, cot[:, span], (((1,), (1,)), ((), ())), preferred_element_type=F32
        )
        send[place, :, 0:width] = term_a.astype(BF)
        send[place, :, width:width + units] = term_b.astype(BF)
        up = factors[place][:, width:width + units]
        delta[:, span] = 2.0 * lax.dot_general(
            up, inputs, (((0,), (0,)), ((), ())), preferred_element_type=F32
        )


def sum_kernel(me, used, terms, grad_a, grad_b):
    groups, slots = used.shape
    per_owner, rank, width = grad_a.shape
    units = grad_b.shape[2]
    grad_a[...] = jnp.zeros(grad_a.shape, F32)
    grad_b[...] = jnp.zeros(grad_b.shape, F32)
    for group in range(groups):
        low, high = pair_of(used, group, me[0], per_owner, slots)

        @pl.when(high >= 0)
        def _():
            for place, local in ((0, low), (1, high)):
                grad_a[local] += terms[group, place, :, 0:width].astype(F32)
                grad_b[local] += terms[group, place, :, width:width + units].astype(F32)


def times_rows(meta, got, swapped, tokens):
    span = got.shape[1]
    core = meta[1]
    total = None
    for source, block in ((got, core), (swapped, 1 - core)):
        place = pl.ds(pl.multiple_of(block * span, span), span)
        term = lax.dot_general(
            source[...], tokens[:, place], (((1,), (1,)), ((), ())), preferred_element_type=F32
        )
        total = term if total is None else total + term
    return total


def shared_kernel(meta, got2, swap2, got1, swap1, got3, swap3, tokens, *outs):
    far_up, far_down, up_soon, down_soon, up_late, down_late = outs
    half = far_up.shape[0]
    far = times_rows(meta, got2, swap2, tokens)
    far_up[...] = far[:half].astype(BF)
    far_down[...] = far[half:].astype(BF)
    near = times_rows(meta, got1, swap1, tokens)
    up_late[...] = near[:half]
    up_soon[...] = near[half:].astype(BF)
    near = times_rows(meta, got3, swap3, tokens)
    down_soon[...] = near[:half].astype(BF)
    down_late[...] = near[half:]


def own_kernel(meta, *refs):
    weights, tokens, delta, out, rows = refs[:-4], *refs[-4:]
    width = weights[0].shape[1]

    @pl.when(pl.program_id(0) == 0)
    def _():
        for block, source in enumerate(weights):
            rows[:, block * width:(block + 1) * width] = source[...]

    out[...] = delta[...] + lax.dot_general(
        rows[...], tokens[...], (((1,), (1,)), ((), ())), preferred_element_type=F32
    )


def fetch_kernel(meta, *refs):
    for source, out in zip(refs[:3], refs[3:]):
        out[...] = source[...]


def join_kernel(base, up_late, up_soon, down_soon, down_late, out):
    half = up_late.shape[0]
    out[0:half, :] = (
        base[0:half, :] + up_late[...].astype(F32) + down_soon[...].astype(F32)
    ).astype(BF)
    out[half:, :] = (
        base[half:, :] + up_soon[...].astype(F32) + down_late[...].astype(F32)
    ).astype(BF)


def call(kernel, outs, specs, scratch=(), limit=8):
    return pl.pallas_call(
        kernel,
        out_shape=outs,
        in_specs=specs,
        out_specs=jax.tree.map(lambda _: VMEM, outs),
        scratch_shapes=scratch,
        compiler_params=pltpu.CompilerParams(vmem_limit_bytes=limit * 1024 * 1024),
    )


def hop(value, axis, step):
    n = lax.axis_size(axis)
    return lax.ppermute(value, axis, [(i, (i + step) % n) for i in range(n)])


def on_device(tokens, cotangent, weight, down, up, used, order):
    n_y, n_z = lax.axis_size("y"), lax.axis_size("z")
    owners = lax.axis_size(DP)
    members = n_y * n_z
    rows, width = tokens.shape
    units = weight.shape[1]
    per_owner, _, rank = down.shape
    packed = -(-(width + units) // 128) * 128
    me = lax.axis_index(DP)
    whole = jax.ShapeDtypeStruct

    together = lax.optimization_barrier
    x, core, z, y = (lax.axis_index(name) for name in ("x", "core", "z", "y"))
    meta = jnp.stack([x, core, z, y]).astype(jnp.int32)
    me_arr = me.reshape(1).astype(jnp.int32)

    gathered = lax.all_gather(tokens, "z", axis=1, tiled=True)

    weight_t = weight.T
    span = n_z // 2

    def block_for(r):
        return lambda i, meta: (
            0, (span * meta[1] + i) * n_y + lax.rem(meta[3] + n_y - r, jnp.int32(n_y))
        )

    fetched = pl.pallas_call(
        fetch_kernel,
        out_shape=[whole((units, span * width), BF)] * 3,
        grid_spec=pltpu.PrefetchScalarGridSpec(
            num_scalar_prefetch=1,
            grid=(span,),
            in_specs=[pl.BlockSpec((units, width), block_for(r)) for r in (1, 2, 3)],
            out_specs=[pl.BlockSpec((units, width), lambda i, meta: (0, i))] * 3,
        ),
    )(meta, weight_t, weight_t, weight_t)

    down_t = jnp.transpose(down, (0, 2, 1))
    used_all = lax.all_to_all(
        jnp.broadcast_to(used[None], (owners,) + used.shape), DP, 0, 0, tiled=True
    ).reshape(owners, used.shape[1])
    picked = call(pick_kernel, whole((owners, 2, rank, packed), BF), [SMEM, SMEM, VMEM, VMEM])(
        me_arr, used_all, down_t, up
    )
    picked, fetched = together((picked, fetched))
    pieces = tuple(hop(item, "y", -r) for r, item in zip((1, 2, 3), fetched))
    factors = lax.all_to_all(picked, DP, 0, 0, tiled=True).reshape(owners * 2, rank, packed)
    cot_t = cotangent.T
    sizes = dict(rank=rank, width=width, units=units)
    part = call(
        functools.partial(parts_kernel, **sizes),
        whole((rows, 2 * rank), BF),
        [SMEM, SMEM, VMEM, VMEM, VMEM],
    )(used, order, factors, tokens, cot_t)
    share = rows // members
    parts = lax.all_to_all(part.reshape(members, share, 2 * rank), MP, 0, 0, tiled=True)
    summed = jnp.sum(parts.astype(F32), axis=0).astype(BF)
    summed, pieces = together((summed, pieces))
    swapped = tuple(hop(item, "core", 1) for item in pieces)
    both = lax.all_to_all(
        jnp.broadcast_to(summed[None], (members,) + summed.shape), MP, 0, 0, tiled=True
    ).reshape(rows, 2 * rank)

    half, step = units // 2, 256
    side = span * width
    narrow = pltpu.HBM((half, rows), BF)
    part_block = pl.BlockSpec((half, step), lambda i, meta: (0, i))
    full_block = pl.BlockSpec((units, step), lambda i, meta: (0, i))
    token_block = pl.BlockSpec((step, n_z * width), lambda i, meta: (i, 0))
    all_rows = pl.BlockSpec((units, side), lambda i, meta: (0, 0))

    def over_tokens(kernel, outs, ins, out_specs, scratch, work=1):
        return pl.pallas_call(
            kernel,
            out_shape=outs,
            grid_spec=pltpu.PrefetchScalarGridSpec(
                num_scalar_prefetch=1,
                grid=(rows // step,),
                in_specs=ins,
                out_specs=out_specs,
                scratch_shapes=scratch,
            ),
            compiler_params=pltpu.CompilerParams(vmem_limit_bytes=48 * 1024 * 1024),
            cost_estimate=pl.CostEstimate(flops=work, bytes_accessed=work, transcendentals=0),
        )

    got1, got2, got3 = pieces
    swap1, swap2, swap3 = swapped
    broad = pltpu.HBM((half, rows), F32)
    far_up, far_down, up_soon, down_soon, up_late, down_late = over_tokens(
        shared_kernel,
        [narrow] * 4 + [broad] * 2,
        [all_rows] * 6 + [token_block],
        [part_block] * 6,
        [],
    )(meta, got2, swap2, got1, swap1, got3, swap3, gathered)
    both, far_up, far_down = together((both, far_up, far_down))
    far_up, far_down = hop(far_up, "y", 1), hop(far_down, "y", -1)
    up_soon, down_soon = hop(up_soon, "y", 1), hop(down_soon, "y", -1)
    up_late = hop((up_late + far_up.astype(F32)).astype(BF), "y", 1)
    down_late = hop((down_late + far_down.astype(F32)).astype(BF), "y", -1)

    send, delta = call(
        functools.partial(grads_kernel, **sizes),
        (whole((owners * 2, rank, packed), BF), whole((units, rows), F32)),
        [SMEM, SMEM, VMEM, VMEM, VMEM, VMEM],
    )(used, order, factors, tokens, cot_t, both)
    terms = lax.all_to_all(send.reshape(owners, 2, rank, packed), DP, 0, 0, tiled=True)
    grad_a, grad_b = call(
        sum_kernel,
        (whole((per_owner, rank, width), F32), whole((per_owner, rank, units), F32)),
        [SMEM, SMEM, VMEM],
    )(me_arr, used_all, terms)

    def own_block(block):
        return pl.BlockSpec((units, width), lambda i, meta: (0, block * n_y + meta[3]))

    base = over_tokens(
        own_kernel,
        whole((units, rows), F32),
        [own_block(block) for block in range(n_z)] + [token_block, full_block],
        full_block,
        [pltpu.VMEM((units, n_z * width), BF)],
        work=20_000_000_000,
    )(meta, *[weight_t] * n_z, gathered, delta)
    out = call(join_kernel, whole((units, rows), BF), [VMEM] * 5)(
        base, up_late, up_soon, down_soon, down_late
    )
    return out.T, jnp.transpose(grad_a, (0, 2, 1)), grad_b


def solution(mesh):
    grid = Mesh(mesh.devices.reshape(4, 2, 8, 4), ("x", "core", "z", "y"))
    return jax.shard_map(
        on_device,
        mesh=grid,
        in_specs=(
            P(DP, MP),
            P(DP, MP),
            P(None, MP),
            P(DP, MP, None),
            P(DP, None, MP),
            P(DP, None),
            P(DP, None),
        ),
        out_specs=(P(DP, MP), P(DP, MP, None), P(DP, None, MP)),
        check_vma=False,
    )
```

```python
import functools

import jax
import jax.numpy as jnp
from jax import lax
from jax.experimental import pallas as pl
from jax.experimental.pallas import tpu as pltpu
from jax.sharding import Mesh, PartitionSpec as P

BF = jnp.bfloat16
F32 = jnp.float32
DP = ("x", "core")
MP = ("z", "y")
VMEM = pl.BlockSpec(memory_space=pltpu.VMEM)
SMEM = pl.BlockSpec(memory_space=pltpu.SMEM)


def pair_of(used, group, owner, per_owner, slots):
    low, high = jnp.int32(per_owner), jnp.int32(-1)
    for slot in range(slots):
        local = used[group, slot] - owner * per_owner
        inside = jnp.logical_and(local >= 0, local < per_owner)
        low = jnp.where(inside, jnp.minimum(low, local), low)
        high = jnp.where(inside, jnp.maximum(high, local), high)
    return low, high


def place_of(used, order, sequence, per_owner, slots):
    adapter = used[0, order[0, sequence]]
    owner = lax.div(adapter, jnp.int32(per_owner))
    second = jnp.int32(0)
    for slot in range(slots):
        other = used[0, slot]
        same = jnp.logical_and(lax.div(other, jnp.int32(per_owner)) == owner, other < adapter)
        second = jnp.where(same, jnp.int32(1), second)
    return owner * 2 + second


def pick_kernel(me, used, down, up, out):
    groups, slots = used.shape
    per_owner, rank, width = down.shape
    units = up.shape[2]
    for group in range(groups):
        low, high = pair_of(used, group, me[0], per_owner, slots)
        for place, local in ((0, low), (1, high)):
            index = jnp.clip(local, 0, per_owner - 1)
            out[group, place, :, 0:width] = down[index]
            out[group, place, :, width:width + units] = up[index]
            out[group, place, :, width + units:] = jnp.zeros((rank, out.shape[3] - width - units), BF)


def parts_kernel(used, order, factors, tokens, cot, out, *, rank, width, units):
    sequences = order.shape[1]
    length = tokens.shape[0] // sequences
    per_owner = sequences
    for i in range(sequences):
        place = place_of(used, order, i, per_owner, used.shape[1])
        own = factors[place]
        rows = tokens[i * length:(i + 1) * length, :]
        inputs = lax.dot_general(
            own[:, 0:width], rows, (((1,), (1,)), ((), ())), preferred_element_type=F32
        )
        back = 2.0 * jnp.dot(
            own[:, width:width + units],
            cot[:, i * length:(i + 1) * length],
            preferred_element_type=F32,
        )
        both = jnp.concatenate([inputs, back], axis=0)
        out[i * length:(i + 1) * length, :] = both.T.astype(BF)


def grads_kernel(used, order, tokens, cot, both, send, *, rank, width, units):
    sequences = order.shape[1]
    length = tokens.shape[0] // sequences
    per_owner = sequences
    send[...] = jnp.zeros(send.shape, BF)
    for i in range(sequences):
        place = place_of(used, order, i, per_owner, used.shape[1])
        span = slice(i * length, (i + 1) * length)
        turned = both[span, :].astype(F32).T.astype(BF)
        inputs, back = turned[0:rank, :], turned[rank:2 * rank, :]
        term_a = jnp.dot(back, tokens[span, :], preferred_element_type=F32)
        term_b = 2.0 * lax.dot_general(
            inputs, cot[:, span], (((1,), (1,)), ((), ())), preferred_element_type=F32
        )
        send[place, :, 0:width] = term_a.astype(BF)
        send[place, :, width:width + units] = term_b.astype(BF)


def sum_kernel(me, used, terms, grad_a, grad_b):
    groups, slots = used.shape
    per_owner, rank, width = grad_a.shape
    units = grad_b.shape[2]
    grad_a[...] = jnp.zeros(grad_a.shape, F32)
    grad_b[...] = jnp.zeros(grad_b.shape, F32)
    for group in range(groups):
        low, high = pair_of(used, group, me[0], per_owner, slots)

        @pl.when(high >= 0)
        def _():
            for place, local in ((0, low), (1, high)):
                grad_a[local] += terms[group, place, :, 0:width].astype(F32)
                grad_b[local] += terms[group, place, :, width:width + units].astype(F32)


def join_rows(meta, tokens, wide):
    own, f1, b1, f2, b2, f3, b3, f4, b4 = tokens
    width = own.shape[1]
    first = pl.program_id(0) < pl.num_programs(0) // 2
    for step, block in ((0, own[...]), (1, b1[...]), (2, b2[...]), (3, b3[...]),
                        (4, jnp.where(first, f4[...], b4[...])),
                        (5, f3[...]), (6, f2[...]), (7, f1[...])):
        place = lax.rem(meta[2] + step, jnp.int32(8)) * width
        wide[:, pl.ds(pl.multiple_of(place, width), width)] = block


def times_rows(meta, got, swapped, tokens):
    span = got.shape[1]
    core = meta[1]
    total = None
    for source, block in ((got, core), (swapped, 1 - core)):
        place = pl.ds(pl.multiple_of(block * span, span), span)
        term = lax.dot_general(
            source[...], tokens[:, place], (((1,), (1,)), ((), ())), preferred_element_type=F32
        )
        total = term if total is None else total + term
    return total


def shared_kernel(meta, got2, swap2, got1, swap1, got3, swap3, *refs):
    far_up, far_down, up_soon, down_soon, up_late, down_late, tokens = refs[9:]
    half = far_up.shape[0]
    join_rows(meta, refs[:9], tokens)
    far = times_rows(meta, got2, swap2, tokens)
    far_up[...] = far[:half].astype(BF)
    far_down[...] = far[half:].astype(BF)
    near = times_rows(meta, got1, swap1, tokens)
    up_late[...] = near[:half]
    up_soon[...] = near[half:].astype(BF)
    near = times_rows(meta, got3, swap3, tokens)
    down_soon[...] = near[:half].astype(BF)
    down_late[...] = near[half:]


def own_kernel(meta, used, order, *refs):
    weights, blocks, factors = refs[:8], refs[8:17], refs[17:-4]
    both, out, rows, tokens = refs[-4:]
    width = weights[0].shape[1]
    units = rows.shape[0]
    join_rows(meta, blocks, tokens)

    @pl.when(pl.program_id(0) == 0)
    def _():
        for block, source in enumerate(weights):
            rows[:, block * width:(block + 1) * width] = source[...]

    base = lax.dot_general(
        rows[...], tokens[...], (((1,), (1,)), ((), ())), preferred_element_type=F32
    )
    length = both.shape[0] // len(factors)
    for k, adapter in enumerate(factors):
        span = slice(k * length, (k + 1) * length)
        rank = adapter.shape[1]
        inputs = both[span, :].astype(F32).T.astype(BF)[0:rank, :]
        delta = lax.dot_general(
            adapter[0, :, width:width + units], inputs, (((0,), (0,)), ((), ())),
            preferred_element_type=F32,
        )
        out[:, span] = base[:, span] + 2.0 * delta


def fetch_kernel(meta, weight, *refs):
    outs, sems = refs[:3], refs[3]
    width = outs[0].shape[1] // 4
    copies = []
    for r in (1, 2, 3):
        to = lax.rem(meta[3] + 4 - r, jnp.int32(4))
        for i in range(4):
            place = ((4 * meta[1] + i) * 4 + to) * width
            copies.append(pltpu.make_async_copy(
                weight.at[:, pl.ds(pl.multiple_of(place, width), width)],
                outs[r - 1].at[:, i * width:(i + 1) * width],
                sems.at[4 * (r - 1) + i],
            ))
    for copy in copies:
        copy.start()
    for copy in copies:
        copy.wait()


def late_kernel(up, far_up, down, far_down, out_up, out_down):
    out_up[...] = (up[...] + far_up[...].astype(F32)).astype(BF)
    out_down[...] = (down[...] + far_down[...].astype(F32)).astype(BF)


def join_kernel(base, up_late, up_soon, down_soon, down_late, out):
    half = up_late.shape[0]
    out[0:half, :] = (
        base[0:half, :] + up_late[...].astype(F32) + down_soon[...].astype(F32)
    ).astype(BF)
    out[half:, :] = (
        base[half:, :] + up_soon[...].astype(F32) + down_late[...].astype(F32)
    ).astype(BF)


def call(kernel, outs, specs, scratch=(), limit=8):
    return pl.pallas_call(
        kernel,
        out_shape=outs,
        in_specs=specs,
        out_specs=jax.tree.map(lambda _: VMEM, outs),
        scratch_shapes=scratch,
        compiler_params=pltpu.CompilerParams(vmem_limit_bytes=limit * 1024 * 1024),
    )


def in_hbm(value):
    return pltpu.with_memory_space_constraint(value, pltpu.HBM)


def hop(value, axis, step):
    n = lax.axis_size(axis)
    return lax.ppermute(value, axis, [(i, (i + step) % n) for i in range(n)])


def on_device(tokens, cotangent, weight, down, up, used, order):
    n_y, n_z = lax.axis_size("y"), lax.axis_size("z")
    owners = lax.axis_size(DP)
    members = n_y * n_z
    rows, width = tokens.shape
    units = weight.shape[1]
    per_owner, _, rank = down.shape
    packed = -(-(width + units) // 128) * 128
    me = lax.axis_index(DP)
    whole = jax.ShapeDtypeStruct

    together = lax.optimization_barrier
    x, core, z, y = (lax.axis_index(name) for name in ("x", "core", "z", "y"))
    meta = jnp.stack([x, core, z, y]).astype(jnp.int32)
    me_arr = me.reshape(1).astype(jnp.int32)

    f1, b1 = hop(tokens, "z", 1), hop(tokens, "z", -1)

    weight_t = weight.T
    span = n_z // 2

    anywhere = pl.BlockSpec(memory_space=pl.ANY)
    fetched = pl.pallas_call(
        fetch_kernel,
        out_shape=[whole((units, span * width), BF)] * 3,
        in_specs=[SMEM, anywhere],
        out_specs=[VMEM] * 3,
        scratch_shapes=[pltpu.SemaphoreType.DMA((12,))],
    )(meta, weight_t)

    down_t = jnp.transpose(down, (0, 2, 1))
    used_all = lax.all_to_all(
        jnp.broadcast_to(used[None], (owners,) + used.shape), DP, 0, 0, tiled=True
    ).reshape(owners, used.shape[1])
    picked = call(pick_kernel, whole((owners, 2, rank, packed), BF), [SMEM, SMEM, VMEM, VMEM])(
        me_arr, used_all, down_t, up
    )
    picked, fetched, f1, b1 = together((picked, fetched, f1, b1))
    pieces = tuple(hop(item, "y", -r) for r, item in zip((1, 2, 3), fetched))
    factors = lax.all_to_all(picked, DP, 0, 0, tiled=True).reshape(owners * 2, rank, packed)
    f2, b2 = hop(f1, "z", 1), hop(b1, "z", -1)
    factors, f2, b2 = (factors, f2, b2)
    f3, b3 = hop(f2, "z", 1), hop(b2, "z", -1)
    half_rows = rows // 2
    f4, b4 = hop(f3[:half_rows], "z", 1), hop(b3[half_rows:], "z", -1)
    cot_t = cotangent.T
    sizes = dict(rank=rank, width=width, units=units)
    part = call(
        functools.partial(parts_kernel, **sizes),
        whole((rows, 2 * rank), BF),
        [SMEM, SMEM, VMEM, VMEM, VMEM],
    )(used, order, factors, tokens, cot_t)
    share = rows // members
    parts = lax.all_to_all(part.reshape(members, share, 2 * rank), MP, 0, 0, tiled=True)
    summed = jnp.sum(parts.astype(F32), axis=0).astype(BF)
    summed, pieces, f4, b4 = together((summed, pieces, f4, b4))
    gathered = (tokens, f1, b1, f2, b2, f3, b3, f4, b4)
    swapped = tuple(hop(item, "core", 1) for item in pieces)
    both = lax.all_to_all(
        jnp.broadcast_to(summed[None], (members,) + summed.shape), MP, 0, 0, tiled=True
    ).reshape(rows, 2 * rank)

    half, step = units // 2, 256
    steps = rows // step
    side = span * width
    narrow = pltpu.HBM((half, rows), BF)
    part_block = pl.BlockSpec((half, step), lambda i, *_: (0, i))
    full_block = pl.BlockSpec((units, step), lambda i, *_: (0, i))
    token_block = pl.BlockSpec((step, width), lambda i, *_: (i, 0))
    early_block = pl.BlockSpec((step, width), lambda i, *_: (jnp.minimum(i, steps // 2 - 1), 0))
    late_block = pl.BlockSpec((step, width), lambda i, *_: (jnp.maximum(i - steps // 2, 0), 0))
    token_blocks = [token_block] * 7 + [early_block, late_block]
    wide = pltpu.VMEM((step, n_z * width), BF)
    all_rows = pl.BlockSpec((units, side), lambda i, *_: (0, 0))

    def over_tokens(kernel, outs, ins, out_specs, scratch, work=1, scalars=1):
        return pl.pallas_call(
            kernel,
            out_shape=outs,
            grid_spec=pltpu.PrefetchScalarGridSpec(
                num_scalar_prefetch=scalars,
                grid=(steps,),
                in_specs=ins,
                out_specs=out_specs,
                scratch_shapes=scratch,
            ),
            compiler_params=pltpu.CompilerParams(vmem_limit_bytes=48 * 1024 * 1024),
            cost_estimate=pl.CostEstimate(flops=work, bytes_accessed=work, transcendentals=0),
        )

    got1, got2, got3 = pieces
    swap1, swap2, swap3 = swapped
    broad = pltpu.HBM((half, rows), F32)
    far_up, far_down, up_soon, down_soon, up_late, down_late = over_tokens(
        shared_kernel,
        [narrow] * 4 + [broad] * 2,
        [all_rows] * 6 + token_blocks,
        [part_block] * 6,
        [wide],
    )(meta, got2, swap2, got1, swap1, got3, swap3, *gathered)
    both = together((both, far_up, far_down))[0]
    far_up, far_down = hop(far_up, "y", 1), hop(far_down, "y", -1)
    up_soon, down_soon = hop(up_soon, "y", 1), hop(down_soon, "y", -1)
    up_late, down_late = call(late_kernel, (narrow, narrow), [VMEM] * 4)(
        in_hbm(up_late), far_up, in_hbm(down_late), far_down
    )
    up_late, down_late = hop(up_late, "y", 1), hop(down_late, "y", -1)

    send = call(
        functools.partial(grads_kernel, **sizes),
        pltpu.HBM((owners * 2, rank, packed), BF),
        [SMEM, SMEM, VMEM, VMEM, VMEM],
    )(used, order, tokens, cot_t, both)
    terms = lax.all_to_all(send.reshape(owners, 2, rank, packed), DP, 0, 0, tiled=True)
    grad_a, grad_b = call(
        sum_kernel,
        (whole((per_owner, rank, width), F32), whole((per_owner, rank, units), F32)),
        [SMEM, SMEM, VMEM],
    )(me_arr, used_all, terms)

    def own_block(block):
        return pl.BlockSpec((units, width), lambda i, meta, *_: (0, block * n_y + meta[3]))

    slots = used.shape[1]
    together_in_step = step * order.shape[1] // rows

    def adapter_block(k):
        return pl.BlockSpec((1, rank, packed), lambda i, meta, used, order: (
            place_of(used, order, together_in_step * i + k, per_owner, slots), 0, 0
        ))

    base = over_tokens(
        own_kernel,
        whole((units, rows), F32),
        [own_block(block) for block in range(n_z)] + token_blocks
        + [adapter_block(k) for k in range(together_in_step)]
        + [pl.BlockSpec((step, 2 * rank), lambda i, *_: (i, 0))],
        full_block,
        [pltpu.VMEM((units, n_z * width), BF), wide],
        work=20_000_000_000,
        scalars=3,
    )(meta, used, order, *[weight_t] * n_z, *gathered, *[factors] * together_in_step, both)
    base, grad_a, grad_b = together((base, grad_a, grad_b))
    out = call(join_kernel, whole((units, rows), BF), [VMEM] * 5)(
        in_hbm(base), up_late, up_soon, down_soon, down_late
    )
    return out.T, jnp.transpose(grad_a, (0, 2, 1)), grad_b


def solution(mesh):
    grid = Mesh(mesh.devices.reshape(4, 2, 8, 4), ("x", "core", "z", "y"))
    return jax.shard_map(
        on_device,
        mesh=grid,
        in_specs=(
            P(DP, MP),
            P(DP, MP),
            P(None, MP),
            P(DP, MP, None),
            P(DP, None, MP),
            P(DP, None),
            P(DP, None),
        ),
        out_specs=(P(DP, MP), P(DP, MP, None), P(DP, None, MP)),
        check_vma=False,
    )
```

```python
import functools

import jax
import jax.numpy as jnp
from jax import lax
from jax.experimental import pallas as pl
from jax.experimental.pallas import tpu as pltpu
from jax.sharding import Mesh, PartitionSpec as P

BF = jnp.bfloat16
F32 = jnp.float32
DP = ("x", "core")
MP = ("z", "y")
VMEM = pl.BlockSpec(memory_space=pltpu.VMEM)
SMEM = pl.BlockSpec(memory_space=pltpu.SMEM)


def pair_of(used, group, owner, per_owner, slots):
    low, high = jnp.int32(per_owner), jnp.int32(-1)
    for slot in range(slots):
        local = used[group, slot] - owner * per_owner
        inside = jnp.logical_and(local >= 0, local < per_owner)
        low = jnp.where(inside, jnp.minimum(low, local), low)
        high = jnp.where(inside, jnp.maximum(high, local), high)
    return low, high


def place_of(used, order, sequence, per_owner, slots):
    adapter = used[0, order[0, sequence]]
    owner = lax.div(adapter, jnp.int32(per_owner))
    second = jnp.int32(0)
    for slot in range(slots):
        other = used[0, slot]
        same = jnp.logical_and(lax.div(other, jnp.int32(per_owner)) == owner, other < adapter)
        second = jnp.where(same, jnp.int32(1), second)
    return owner * 2 + second


def pick_kernel(me, used, down, up, out):
    groups, slots = used.shape
    per_owner, rank, width = down.shape
    units = up.shape[2]
    for group in range(groups):
        low, high = pair_of(used, group, me[0], per_owner, slots)
        for place, local in ((0, low), (1, high)):
            index = jnp.clip(local, 0, per_owner - 1)
            out[group, place, :, 0:width] = down[index]
            out[group, place, :, width:width + units] = up[index]
            out[group, place, :, width + units:] = jnp.zeros((rank, out.shape[3] - width - units), BF)


def parts_kernel(used, order, factors, tokens, cot, out, *, rank, width, units):
    sequences = order.shape[1]
    length = tokens.shape[0] // sequences
    per_owner = sequences
    for i in range(sequences):
        place = place_of(used, order, i, per_owner, used.shape[1])
        own = factors[place]
        rows = tokens[i * length:(i + 1) * length, :]
        inputs = lax.dot_general(
            own[:, 0:width], rows, (((1,), (1,)), ((), ())), preferred_element_type=F32
        )
        back = 2.0 * jnp.dot(
            own[:, width:width + units],
            cot[:, i * length:(i + 1) * length],
            preferred_element_type=F32,
        )
        both = jnp.concatenate([inputs, back], axis=0)
        out[i * length:(i + 1) * length, :] = both.T.astype(BF)


def total_kernel(parts, out):
    total = parts[0].astype(F32)
    for i in range(1, parts.shape[0]):
        total += parts[i].astype(F32)
    for i in range(out.shape[0]):
        out[i] = total


def round_kernel(totals, out):
    total = totals[0]
    for i in range(1, totals.shape[0]):
        total += totals[i]
    for i in range(out.shape[0]):
        out[i] = total.astype(BF)


def grads_kernel(used, order, tokens, cot, both, send, *, rank, width, units):
    sequences = order.shape[1]
    length = tokens.shape[0] // sequences
    per_owner = sequences
    send[...] = jnp.zeros(send.shape, BF)
    for i in range(sequences):
        place = place_of(used, order, i, per_owner, used.shape[1])
        span = slice(i * length, (i + 1) * length)
        turned = both[span, :].astype(F32).T.astype(BF)
        inputs, back = turned[0:rank, :], turned[rank:2 * rank, :]
        term_a = jnp.dot(back, tokens[span, :], preferred_element_type=F32)
        term_b = 2.0 * lax.dot_general(
            inputs, cot[:, span], (((1,), (1,)), ((), ())), preferred_element_type=F32
        )
        send[place, :, 0:width] = term_a.astype(BF)
        send[place, :, width:width + units] = term_b.astype(BF)


def sum_kernel(me, used, terms, grad_a, grad_b):
    groups, slots = used.shape
    per_owner, rank, width = grad_a.shape
    units = grad_b.shape[2]
    grad_a[...] = jnp.zeros(grad_a.shape, F32)
    grad_b[...] = jnp.zeros(grad_b.shape, F32)
    for group in range(groups):
        low, high = pair_of(used, group, me[0], per_owner, slots)

        @pl.when(high >= 0)
        def _():
            for place, local in ((0, low), (1, high)):
                grad_a[local] += terms[group, place, :, 0:width].astype(F32)
                grad_b[local] += terms[group, place, :, width:width + units].astype(F32)


def join_rows(meta, tokens, wide):
    own, f1, b1, f2, b2, f3, b3, f4, b4 = tokens
    width = own.shape[1]
    first = pl.program_id(0) < pl.num_programs(0) // 2
    for step, block in ((0, own[...]), (1, b1[...]), (2, b2[...]), (3, b3[...]),
                        (4, jnp.where(first, f4[...], b4[...])),
                        (5, f3[...]), (6, f2[...]), (7, f1[...])):
        place = lax.rem(meta[2] + step, jnp.int32(8)) * width
        wide[:, pl.ds(pl.multiple_of(place, width), width)] = block


def times_rows(meta, got, swapped, tokens):
    span = got.shape[1]
    core = meta[1]
    total = None
    for source, block in ((got, core), (swapped, 1 - core)):
        place = pl.ds(pl.multiple_of(block * span, span), span)
        term = lax.dot_general(
            source[...], tokens[:, place], (((1,), (1,)), ((), ())), preferred_element_type=F32
        )
        total = term if total is None else total + term
    return total


def shared_kernel(meta, got2, swap2, got1, swap1, got3, swap3, *refs):
    far_up, far_down, up_soon, down_soon, up_late, down_late, tokens = refs[9:]
    half = far_up.shape[0]
    join_rows(meta, refs[:9], tokens)
    far = times_rows(meta, got2, swap2, tokens)
    far_up[...] = far[:half].astype(BF)
    far_down[...] = far[half:].astype(BF)
    near = times_rows(meta, got1, swap1, tokens)
    up_late[...] = near[:half]
    up_soon[...] = near[half:].astype(BF)
    near = times_rows(meta, got3, swap3, tokens)
    down_soon[...] = near[:half].astype(BF)
    down_late[...] = near[half:]


def own_kernel(meta, used, order, *refs):
    weights, blocks, factors = refs[:8], refs[8:17], refs[17:-4]
    both, out, rows, tokens = refs[-4:]
    width = weights[0].shape[1]
    units = rows.shape[0]
    join_rows(meta, blocks, tokens)

    @pl.when(pl.program_id(0) == 0)
    def _():
        for block, source in enumerate(weights):
            rows[:, block * width:(block + 1) * width] = source[...]

    base = lax.dot_general(
        rows[...], tokens[...], (((1,), (1,)), ((), ())), preferred_element_type=F32
    )
    length = both.shape[0] // len(factors)
    for k, adapter in enumerate(factors):
        span = slice(k * length, (k + 1) * length)
        rank = adapter.shape[1]
        inputs = both[span, :].astype(F32).T.astype(BF)[0:rank, :]
        delta = lax.dot_general(
            adapter[0, :, width:width + units], inputs, (((0,), (0,)), ((), ())),
            preferred_element_type=F32,
        )
        out[:, span] = base[:, span] + 2.0 * delta


def fetch_kernel(meta, weight, *refs):
    outs, sems = refs[:3], refs[3]
    width = outs[0].shape[1] // 4
    copies = []
    for r in (1, 2, 3):
        to = lax.rem(meta[3] + 4 - r, jnp.int32(4))
        for i in range(4):
            place = ((4 * meta[1] + i) * 4 + to) * width
            copies.append(pltpu.make_async_copy(
                weight.at[:, pl.ds(pl.multiple_of(place, width), width)],
                outs[r - 1].at[:, i * width:(i + 1) * width],
                sems.at[4 * (r - 1) + i],
            ))
    for copy in copies:
        copy.start()
    for copy in copies:
        copy.wait()


def late_kernel(up, far_up, down, far_down, out_up, out_down):
    out_up[...] = (up[...] + far_up[...].astype(F32)).astype(BF)
    out_down[...] = (down[...] + far_down[...].astype(F32)).astype(BF)


def join_kernel(base, up_late, up_soon, down_soon, down_late, out):
    half = up_late.shape[0]
    out[0:half, :] = (
        base[0:half, :] + up_late[...].astype(F32) + down_soon[...].astype(F32)
    ).astype(BF)
    out[half:, :] = (
        base[half:, :] + up_soon[...].astype(F32) + down_late[...].astype(F32)
    ).astype(BF)


def call(kernel, outs, specs, scratch=(), limit=8):
    return pl.pallas_call(
        kernel,
        out_shape=outs,
        in_specs=specs,
        out_specs=jax.tree.map(lambda _: VMEM, outs),
        scratch_shapes=scratch,
        compiler_params=pltpu.CompilerParams(vmem_limit_bytes=limit * 1024 * 1024),
    )


def in_hbm(value):
    return pltpu.with_memory_space_constraint(value, pltpu.HBM)


def hop(value, axis, step):
    n = lax.axis_size(axis)
    return lax.ppermute(value, axis, [(i, (i + step) % n) for i in range(n)])


def on_device(tokens, cotangent, weight, down, up, used, order):
    n_y, n_z = lax.axis_size("y"), lax.axis_size("z")
    owners = lax.axis_size(DP)
    rows, width = tokens.shape
    units = weight.shape[1]
    per_owner, _, rank = down.shape
    packed = -(-(width + units) // 128) * 128
    me = lax.axis_index(DP)
    whole = jax.ShapeDtypeStruct

    together = lax.optimization_barrier
    x, core, z, y = (lax.axis_index(name) for name in ("x", "core", "z", "y"))
    meta = jnp.stack([x, core, z, y]).astype(jnp.int32)
    me_arr = me.reshape(1).astype(jnp.int32)

    f1, b1 = hop(tokens, "z", 1), hop(tokens, "z", -1)

    weight_t = weight.T
    span = n_z // 2

    anywhere = pl.BlockSpec(memory_space=pl.ANY)
    fetched = pl.pallas_call(
        fetch_kernel,
        out_shape=[whole((units, span * width), BF)] * 3,
        in_specs=[SMEM, anywhere],
        out_specs=[VMEM] * 3,
        scratch_shapes=[pltpu.SemaphoreType.DMA((12,))],
    )(meta, weight_t)

    down_t = jnp.transpose(down, (0, 2, 1))
    used_all = lax.all_to_all(
        jnp.broadcast_to(used[None], (owners,) + used.shape), DP, 0, 0, tiled=True
    ).reshape(owners, used.shape[1])
    picked = call(pick_kernel, whole((owners, 2, rank, packed), BF), [SMEM, SMEM, VMEM, VMEM])(
        me_arr, used_all, down_t, up
    )
    picked, fetched, f1, b1 = together((picked, fetched, f1, b1))
    pieces = tuple(hop(item, "y", -r) for r, item in zip((1, 2, 3), fetched))
    factors = lax.all_to_all(picked, DP, 0, 0, tiled=True).reshape(owners * 2, rank, packed)
    f2, b2 = hop(f1, "z", 1), hop(b1, "z", -1)
    factors, f2, b2 = (factors, f2, b2)
    f3, b3 = hop(f2, "z", 1), hop(b2, "z", -1)
    half_rows = rows // 2
    f4, b4 = hop(f3[:half_rows], "z", 1), hop(b3[half_rows:], "z", -1)
    cot_t = cotangent.T
    sizes = dict(rank=rank, width=width, units=units)
    part = call(
        functools.partial(parts_kernel, **sizes),
        whole((rows, 2 * rank), BF),
        [SMEM, SMEM, VMEM, VMEM, VMEM],
    )(used, order, factors, tokens, cot_t)
    share = rows // n_z
    parts = lax.all_to_all(part.reshape(n_z, share, 2 * rank), "z", 0, 0, tiled=True)
    total = call(total_kernel, whole((n_y, share, 2 * rank), F32), [VMEM])(parts)
    totals = lax.all_to_all(total, "y", 0, 0, tiled=True)
    summed = call(round_kernel, whole((n_z, share, 2 * rank), BF), [VMEM])(totals)
    summed, pieces, f4, b4 = together((summed, pieces, f4, b4))
    gathered = (tokens, f1, b1, f2, b2, f3, b3, f4, b4)
    swapped = tuple(hop(item, "core", 1) for item in pieces)
    both = lax.all_to_all(summed, "z", 0, 0, tiled=True).reshape(rows, 2 * rank)

    half, step = units // 2, 256
    steps = rows // step
    side = span * width
    narrow = pltpu.HBM((half, rows), BF)
    part_block = pl.BlockSpec((half, step), lambda i, *_: (0, i))
    full_block = pl.BlockSpec((units, step), lambda i, *_: (0, i))
    token_block = pl.BlockSpec((step, width), lambda i, *_: (i, 0))
    early_block = pl.BlockSpec((step, width), lambda i, *_: (jnp.minimum(i, steps // 2 - 1), 0))
    late_block = pl.BlockSpec((step, width), lambda i, *_: (jnp.maximum(i - steps // 2, 0), 0))
    token_blocks = [token_block] * 7 + [early_block, late_block]
    wide = pltpu.VMEM((step, n_z * width), BF)
    all_rows = pl.BlockSpec((units, side), lambda i, *_: (0, 0))

    def over_tokens(kernel, outs, ins, out_specs, scratch, work=1, scalars=1):
        return pl.pallas_call(
            kernel,
            out_shape=outs,
            grid_spec=pltpu.PrefetchScalarGridSpec(
                num_scalar_prefetch=scalars,
                grid=(steps,),
                in_specs=ins,
                out_specs=out_specs,
                scratch_shapes=scratch,
            ),
            compiler_params=pltpu.CompilerParams(vmem_limit_bytes=48 * 1024 * 1024),
            cost_estimate=pl.CostEstimate(flops=work, bytes_accessed=work, transcendentals=0),
        )

    got1, got2, got3 = pieces
    swap1, swap2, swap3 = swapped
    broad = pltpu.HBM((half, rows), F32)
    far_up, far_down, up_soon, down_soon, up_late, down_late = over_tokens(
        shared_kernel,
        [narrow] * 4 + [broad] * 2,
        [all_rows] * 6 + token_blocks,
        [part_block] * 6,
        [wide],
    )(meta, got2, swap2, got1, swap1, got3, swap3, *gathered)
    both = together((both, far_up, far_down))[0]
    far_up, far_down = hop(far_up, "y", 1), hop(far_down, "y", -1)
    up_late, down_late = call(late_kernel, (narrow, narrow), [VMEM] * 4)(
        in_hbm(up_late), far_up, in_hbm(down_late), far_down
    )
    up_late, down_late = hop(up_late, "y", 1), hop(down_late, "y", -1)

    send = call(
        functools.partial(grads_kernel, **sizes),
        pltpu.HBM((owners * 2, rank, packed), BF),
        [SMEM, SMEM, VMEM, VMEM, VMEM],
    )(used, order, tokens, cot_t, both)
    send, up_soon, down_soon = together((send, up_soon, down_soon))
    up_soon, down_soon = hop(up_soon, "y", 1), hop(down_soon, "y", -1)
    terms = lax.all_to_all(send.reshape(owners, 2, rank, packed), DP, 0, 0, tiled=True)
    grad_a, grad_b = call(
        sum_kernel,
        (whole((per_owner, rank, width), F32), whole((per_owner, rank, units), F32)),
        [SMEM, SMEM, VMEM],
    )(me_arr, used_all, terms)

    def own_block(block):
        return pl.BlockSpec((units, width), lambda i, meta, *_: (0, block * n_y + meta[3]))

    slots = used.shape[1]
    together_in_step = step * order.shape[1] // rows

    def adapter_block(k):
        return pl.BlockSpec((1, rank, packed), lambda i, meta, used, order: (
            place_of(used, order, together_in_step * i + k, per_owner, slots), 0, 0
        ))

    base = over_tokens(
        own_kernel,
        whole((units, rows), F32),
        [own_block(block) for block in range(n_z)] + token_blocks
        + [adapter_block(k) for k in range(together_in_step)]
        + [pl.BlockSpec((step, 2 * rank), lambda i, *_: (i, 0))],
        full_block,
        [pltpu.VMEM((units, n_z * width), BF), wide],
        work=20_000_000_000,
        scalars=3,
    )(meta, used, order, *[weight_t] * n_z, *gathered, *[factors] * together_in_step, both)
    base, grad_a, grad_b = together((base, grad_a, grad_b))
    out = call(join_kernel, whole((units, rows), BF), [VMEM] * 5)(
        in_hbm(base), up_late, up_soon, down_soon, down_late
    )
    return out.T, jnp.transpose(grad_a, (0, 2, 1)), grad_b


def solution(mesh):
    grid = Mesh(mesh.devices.reshape(4, 2, 8, 4), ("x", "core", "z", "y"))
    return jax.shard_map(
        on_device,
        mesh=grid,
        in_specs=(
            P(DP, MP),
            P(DP, MP),
            P(None, MP),
            P(DP, MP, None),
            P(DP, None, MP),
            P(DP, None),
            P(DP, None),
        ),
        out_specs=(P(DP, MP), P(DP, MP, None), P(DP, None, MP)),
        check_vma=False,
    )
```
